128 devices in a mesh: rep: 8 (over x_lo, z), tp: 16 (over y, x_hi, core).
Axes of the slice: x: 4 (x_hi: 2, x_lo: 2; x = x_hi * 2 + x_lo), y: 4, z: 4, core: 2. Of those that a mesh axis runs over, the one named last changes fastest.
Arguments:
- query_weight: bfloat16 [8192, 4096], P(('rep', 'tp')), may hold values from -0.0625 to 0.0625
- key_weight: bfloat16 [8192, 512], P(('rep', 'tp')), may hold values from -0.0625 to 0.0625
- value_weight: bfloat16 [8192, 512], P(('rep', 'tp')), may hold values from -0.0625 to 0.0625
- output_weight: bfloat16 [8192, 4096], P(('rep', 'tp')), may hold values from -0.375 to 0.375
- query_amax: float32 [4096], replicated, may hold values from 0.5 to 20
- key_amax: float32 [512], replicated, may hold values from 0.5 to 20
- hidden: bfloat16 [2560, 2, 8192], P('rep'), may hold values from -6 to 6
- positions: int32 [2560], P('rep'), may hold values from 0 to 2046
- cache_keys: bfloat16 [2560, 4, 256, 128], P(('rep', 'tp')), may hold values from -60 to 60
- cache_values: bfloat16 [2560, 4, 256, 128], P(('rep', 'tp')), may hold values from -6 to 6
- lengths: int32 [2560], P(('rep', 'tp')), may hold values from 1 to 256, as said below
Outputs:
- attn_out: bfloat16 [2560, 2, 8192], P('rep', None, 'tp')
The draws below stay inside these ranges and needn't reach their ends.
Inputs may be any that keep to these rules, and one draw needn't show every extreme that they name: `lengths`: in each aligned block of 20 sequences the first has 256 live slots.
All inputs are finite; a program needn't handle non-finite values.
Results may differ from the reference program's by a relative error of at most 0.0095.
Values may be sent and summed in bfloat16 or wider, within the bound.
A program may use at most 128 MiB of HBM per device.

```python
import math
import jax
import jax.numpy as jnp
from jax import lax

D = 8192
HQ = 32
KVH = 4
HD = 128
LMAX = 256
TOTAL_SEQS = 2560
HELD_SEQS = 20


def draw_cache_keys(key, part):
    key = jax.random.fold_in(key, 23)
    full_shape = (TOTAL_SEQS, KVH, LMAX, HD)
    return jnp.clip(3.0 * jax.random.normal(key, full_shape, jnp.float32), -18.0, 18.0).astype(jnp.bfloat16)


def draw_lengths(key, part):
    key = jax.random.fold_in(key, 11)
    sampled = jax.random.randint(key, (TOTAL_SEQS,), 1, LMAX + 1)
    slot_index = jnp.arange(TOTAL_SEQS) % HELD_SEQS
    return jnp.where(slot_index == 0, LMAX, sampled).astype(jnp.int32)


def plant(result, own_key, smallest, high):
    dims = result.shape
    index_at = [jax.random.randint(jax.random.fold_in(own_key, axis), (), 0, dims[axis]) for axis in range(len(dims))]
    result = result.at[tuple(index_at)].set(smallest)
    longest = dims.index(max(dims))
    index_at[longest] = (index_at[longest] + 1) % dims[longest]
    return result.at[tuple(index_at)].set(high)


def levels(key, shape, cuts, low, top_value):
    gain, own = 1.0, jax.random.fold_in(key, 6)
    for dim, shards_of in cuts:
        heights = jnp.exp(jax.random.uniform(jax.random.fold_in(own, dim), (shards_of,), jnp.float32, low / len(cuts), top_value / len(cuts)))
        gain = gain * jnp.repeat(heights, shape[dim] // shards_of).reshape([-1 if axis == dim else 1 for axis in range(len(shape))])
    return gain


def centred(stream_key, extent, deviation, limit, split=(), kind=jnp.bfloat16):
    level = levels(stream_key, extent, split, -0.22, 0.18) if split else 1.0
    array = jax.random.normal(stream_key, extent, jnp.float32) * deviation * level
    return jnp.minimum(jnp.maximum(array, -limit), limit).astype(kind)


def setup_inputs(seed: int = 0) -> dict:
    splits = jax.random.split(jax.random.key(seed), 12)
    query_weight = centred(splits[0], (D, HQ * HD), D ** -0.5, 0.0625, ((0, 128),))
    key_weight = centred(splits[1], (D, KVH * HD), D ** -0.5, 0.0625, ((0, 128),))
    value_weight = centred(splits[2], (D, KVH * HD), D ** -0.5, 0.0625, ((0, 128),))
    output_weight = centred(splits[3], (D, HQ * HD), (HQ * HD // 16) ** -0.5, 0.375, ((0, 128),))
    query_amax = jnp.clip(jnp.exp(jax.random.uniform(splits[4], (HQ * HD,), jnp.float32, math.log(0.5), math.log(20.0))), 0.5, 20.0)
    key_amax = jnp.clip(jnp.exp(jax.random.uniform(splits[5], (KVH * HD,), jnp.float32, math.log(0.5), math.log(20.0))), 0.5, 20.0)
    hidden = centred(splits[6], (TOTAL_SEQS, 2, D), 1.0, 6.0, ((0, 8),))
    positions = plant(jax.random.randint(splits[7], (TOTAL_SEQS,), 0, 2047), jax.random.fold_in(splits[7], 1), 0, 2046).astype(jnp.int32)
    cache_keys = draw_cache_keys(jax.random.fold_in(splits[11], 71), 0)
    cache_values = centred(splits[9], (TOTAL_SEQS, KVH, LMAX, HD), 1.0, 6.0, ((0, 128),))
    lengths = draw_lengths(jax.random.fold_in(splits[11], 71), 0)
    return dict(query_weight=query_weight, key_weight=key_weight, value_weight=value_weight, output_weight=output_weight, query_amax=query_amax, key_amax=key_amax, hidden=hidden, positions=positions, cache_keys=cache_keys, cache_values=cache_values, lengths=lengths)


ROPE_THETA = 1000000.0

def smoothing(query_amax, key_amax):
    group_size = HQ // KVH
    half_width = HD // 2
    query_peak = lax.optimization_barrier(jnp.max(query_amax.reshape(KVH, group_size, 2, half_width), axis=(1, 2)))
    key_peak = lax.optimization_barrier(jnp.max(key_amax.reshape(KVH, 2, half_width), axis=1))
    factor = jnp.sqrt(key_peak / query_peak)
    return jnp.concatenate([factor, factor], axis=1)

def rotary(vectors, angles):
    half_width = vectors.shape[-1] // 2
    first_half = vectors[..., :half_width]
    second = vectors[..., half_width:]
    cosine = jnp.cos(angles)
    sine_part = jnp.sin(angles)
    return jnp.concatenate([first_half * cosine - second * sine_part, second * cosine + first_half * sine_part], axis=-1)

def attend(queries, fresh_keys, fresh_values, cache_keys, cache_values, lengths):
    block_seqs = queries.shape[0]
    group_size = HQ // KVH
    score_scale = HD ** (-0.5)
    grouped = queries.astype(jnp.float32).reshape(block_seqs, 2, KVH, group_size, HD)
    cache_scores = jnp.einsum('btghd,bgld->btghl', grouped, cache_keys.astype(jnp.float32)) * score_scale
    fresh_scores = jnp.einsum('btghd,bugd->btghu', grouped, fresh_keys.astype(jnp.float32)) * score_scale
    slot_index = jnp.arange(cache_keys.shape[2], dtype=jnp.int32)
    live_slots = slot_index[None, :] < lengths[:, None]
    cache_scores = jnp.where(live_slots[:, None, None, None, :], cache_scores, -jnp.inf)
    token_index = jnp.arange(2, dtype=jnp.int32)
    earlier = token_index[None, :] <= token_index[:, None]
    fresh_scores = jnp.where(earlier[None, :, None, None, :], fresh_scores, -jnp.inf)
    row_max = jnp.maximum(lax.optimization_barrier(jnp.max(cache_scores, axis=-1)), lax.optimization_barrier(jnp.max(fresh_scores, axis=-1)))
    cache_probs = jnp.exp(cache_scores - row_max[..., None])
    fresh_probs = jnp.exp(fresh_scores - row_max[..., None])
    weight_sum = lax.optimization_barrier(jnp.sum(cache_probs, axis=-1)) + lax.optimization_barrier(jnp.sum(fresh_probs, axis=-1))
    cache_round = lax.optimization_barrier(cache_probs.astype(jnp.bfloat16)).astype(jnp.float32)
    fresh_round = lax.optimization_barrier(fresh_probs.astype(jnp.bfloat16)).astype(jnp.float32)
    mixed_sum = jnp.einsum('btghl,bgld->btghd', cache_round, cache_values.astype(jnp.float32))
    mixed_sum = mixed_sum + jnp.einsum('btghu,bugd->btghd', fresh_round, fresh_values.astype(jnp.float32))
    return (mixed_sum / weight_sum[..., None]).astype(jnp.bfloat16).reshape(block_seqs, 2, HQ * HD)

def reference(query_weight, key_weight, value_weight, output_weight, query_amax, key_amax, hidden, positions, cache_keys, cache_values, lengths):
    group_size = HQ // KVH
    factor = smoothing(query_amax, key_amax)
    query_fold = (query_weight.astype(jnp.float32).reshape(D, KVH, group_size, HD) * factor[None, :, None, :]).astype(jnp.bfloat16).reshape(D, HQ * HD)
    key_fold = (key_weight.astype(jnp.float32).reshape(D, KVH, HD) / factor[None]).astype(jnp.bfloat16).reshape(D, KVH * HD)
    seq_count = hidden.shape[0]
    flat_rows = hidden.reshape(seq_count * 2, D)
    query_raw = jnp.dot(flat_rows, query_fold, preferred_element_type=jnp.float32).reshape(seq_count, 2, HQ, HD)
    key_raw = jnp.dot(flat_rows, key_fold, preferred_element_type=jnp.float32).reshape(seq_count, 2, KVH, HD)
    value_new = jnp.dot(flat_rows, value_weight, preferred_element_type=jnp.float32).astype(jnp.bfloat16).reshape(seq_count, 2, KVH, HD)
    token_place = positions[:, None] + jnp.arange(2, dtype=jnp.int32)[None, :]
    freq_index = jnp.arange(HD // 2, dtype=jnp.int32).astype(jnp.float32)
    inverse_freq = ROPE_THETA ** (-2.0 * freq_index / HD)
    angles = token_place.astype(jnp.float32)[:, :, None] * inverse_freq[None, None, :]
    query_rot = rotary(query_raw, angles[:, :, None, :]).astype(jnp.bfloat16)
    key_rot = rotary(key_raw, angles[:, :, None, :]).astype(jnp.bfloat16)
    block_seqs = HELD_SEQS
    block_count = seq_count // block_seqs

    def one_block(pieces):
        return attend(*pieces)
    attended = lax.map(one_block, (query_rot.reshape(block_count, block_seqs, 2, HQ, HD), key_rot.reshape(block_count, block_seqs, 2, KVH, HD), value_new.reshape(block_count, block_seqs, 2, KVH, HD), cache_keys.reshape(block_count, block_seqs, KVH, LMAX, HD), cache_values.reshape(block_count, block_seqs, KVH, LMAX, HD), lengths.reshape(block_count, block_seqs)))
    attended = attended.reshape(seq_count * 2, HQ * HD)
    projected = lax.dot_general(attended, output_weight, (((1,), (1,)), ((), ())), preferred_element_type=jnp.float32)
    return projected.astype(jnp.bfloat16).reshape(seq_count, 2, D)
```

```python
import jax
import jax.numpy as jnp
from jax import lax
from jax.sharding import PartitionSpec as P

HQ = 32
KVH = 4
HD = 128


ROPE_THETA = 1000000.0


def smoothing(query_amax, key_amax):
    group_size = HQ // KVH
    half_width = HD // 2
    query_peak = jnp.max(query_amax.reshape(KVH, group_size, 2, half_width), axis=(1, 2))
    key_peak = jnp.max(key_amax.reshape(KVH, 2, half_width), axis=1)
    factor = jnp.sqrt(key_peak / query_peak)
    return jnp.concatenate([factor, factor], axis=1)


def rotary(vectors, angles):
    half_width = vectors.shape[-1] // 2
    first_half = vectors[..., :half_width]
    second = vectors[..., half_width:]
    cosine = jnp.cos(angles)
    sine_part = jnp.sin(angles)
    return jnp.concatenate(
        [first_half * cosine - second * sine_part, second * cosine + first_half * sine_part],
        axis=-1,
    )


def attend(queries, fresh_keys, fresh_values, cache_keys, cache_values, lengths):
    block_seqs = queries.shape[0]
    group_size = HQ // KVH
    score_scale = HD ** (-0.5)
    grouped = queries.reshape(block_seqs, 2, KVH, group_size, HD)
    cache_scores = (
        jnp.einsum("btghd,bgld->btghl", grouped, cache_keys, preferred_element_type=jnp.float32)
        * score_scale
    )
    fresh_scores = (
        jnp.einsum("btghd,bugd->btghu", grouped, fresh_keys, preferred_element_type=jnp.float32)
        * score_scale
    )
    slot_index = jnp.arange(cache_keys.shape[2], dtype=jnp.int32)
    live_slots = slot_index[None, :] < lengths[:, None]
    cache_scores = jnp.where(live_slots[:, None, None, None, :], cache_scores, -jnp.inf)
    token_index = jnp.arange(2, dtype=jnp.int32)
    earlier = token_index[None, :] <= token_index[:, None]
    fresh_scores = jnp.where(earlier[None, :, None, None, :], fresh_scores, -jnp.inf)
    row_max = jnp.maximum(jnp.max(cache_scores, axis=-1), jnp.max(fresh_scores, axis=-1))
    cache_probs = jnp.exp(cache_scores - row_max[..., None])
    fresh_probs = jnp.exp(fresh_scores - row_max[..., None])
    weight_sum = jnp.sum(cache_probs, axis=-1) + jnp.sum(fresh_probs, axis=-1)
    mixed_sum = jnp.einsum(
        "btghl,bgld->btghd",
        cache_probs.astype(jnp.bfloat16),
        cache_values,
        preferred_element_type=jnp.float32,
    )
    mixed_sum = mixed_sum + jnp.einsum(
        "btghu,bugd->btghd",
        fresh_probs.astype(jnp.bfloat16),
        fresh_values,
        preferred_element_type=jnp.float32,
    )
    return (mixed_sum / weight_sum[..., None]).astype(jnp.bfloat16).reshape(block_seqs, 2, HQ * HD)


def pair_split(matrix, tp_count):
    row_count = matrix.shape[0]
    duplicate = tp_count // KVH
    piece_width = HD // 2 // duplicate
    shaped = matrix.reshape(row_count, KVH, 2, duplicate, piece_width)
    return jnp.swapaxes(shaped, 2, 3).reshape(row_count, tp_count, 2 * piece_width)


def natural_order(pieces, duplicate):
    held_seqs = pieces.shape[0]
    piece_width = pieces.shape[-1] // 2
    shaped = pieces.reshape(held_seqs, KVH, duplicate, 2, 2, piece_width)
    return jnp.transpose(shaped, (0, 3, 1, 4, 2, 5)).reshape(held_seqs, 2, KVH, HD)


def body(
    query_weight,
    key_weight,
    value_weight,
    output_weight,
    query_amax,
    key_amax,
    hidden,
    positions,
    cache_keys,
    cache_values,
    lengths,
):
    tp_count = lax.axis_size("tp")
    rep_count = lax.axis_size("rep")
    tp_rank = lax.axis_index("tp")
    duplicate = tp_count // KVH
    piece_width = HD // 2 // duplicate
    q_width = HQ * HD // tp_count
    kv_width = KVH * HD // tp_count
    heads_here = HQ // tp_count
    split_at = q_width + 2 * kv_width
    factor = smoothing(query_amax, key_amax)
    shard_rows = query_weight.shape[0]
    packed = jnp.concatenate(
        [
            query_weight.reshape(shard_rows, tp_count, -1),
            pair_split(key_weight, tp_count),
            pair_split(value_weight, tp_count),
        ],
        axis=2,
    )
    spread = lax.all_to_all(packed, "tp", split_axis=1, concat_axis=0, tiled=True)
    delivered = lax.all_gather(
        spread.reshape(tp_count * shard_rows, split_at), "rep", axis=0, tiled=True
    )
    model_width = delivered.shape[0]
    routes = [
        (r * tp_count + t, (t % rep_count) * tp_count + (r * tp_count + t) // rep_count)
        for r in range(rep_count)
        for t in range(tp_count)
    ]
    output_local = lax.all_gather(
        lax.ppermute(output_weight, ("rep", "tp"), routes), "rep", axis=0, tiled=True
    )
    group_size = HQ // KVH
    head_factor = lax.dynamic_slice_in_dim(
        jnp.repeat(factor, group_size, axis=0), tp_rank * heads_here, heads_here, 0
    )
    key_factor = lax.dynamic_slice_in_dim(
        pair_split(factor.reshape(1, KVH * HD), tp_count)[0], tp_rank, 1, 0
    )
    query_cols = (
        (
            delivered[:, :q_width].astype(jnp.float32).reshape(model_width, heads_here, HD)
            * head_factor[None]
        )
        .astype(jnp.bfloat16)
        .reshape(model_width, q_width)
    )
    key_cols = (delivered[:, q_width : q_width + kv_width].astype(jnp.float32) / key_factor).astype(
        jnp.bfloat16
    )
    projection = jnp.concatenate(
        [query_cols, key_cols, delivered[:, q_width + kv_width :]], axis=1
    )
    seq_count = hidden.shape[0]
    flat_rows = hidden.reshape(seq_count * 2, model_width)
    projected = jnp.dot(flat_rows, projection, preferred_element_type=jnp.float32)
    token_place = positions[:, None] + jnp.arange(2, dtype=jnp.int32)[None, :]
    place_float = token_place.astype(jnp.float32)[:, :, None]
    query_index = jnp.arange(HD // 2, dtype=jnp.int32).astype(jnp.float32)
    query_freq = ROPE_THETA ** (-2.0 * query_index / HD)
    key_index = (
        tp_rank % duplicate * piece_width + jnp.arange(piece_width, dtype=jnp.int32)
    ).astype(jnp.float32)
    key_freq = ROPE_THETA ** (-2.0 * key_index / HD)
    query_rot = rotary(
        projected[:, :q_width].reshape(seq_count, 2, heads_here, HD),
        (place_float * query_freq)[:, :, None, :],
    ).astype(jnp.bfloat16)
    key_rot = rotary(
        projected[:, q_width : q_width + kv_width].reshape(seq_count, 2, kv_width),
        place_float * key_freq,
    ).astype(jnp.bfloat16)
    value_new = (
        projected[:, q_width + kv_width :].astype(jnp.bfloat16).reshape(seq_count, 2, kv_width)
    )
    outgoing = jnp.concatenate(
        [query_rot.reshape(seq_count, 2, q_width), key_rot, value_new], axis=2
    ).reshape(seq_count, 2 * split_at)
    arrived = lax.all_to_all(outgoing, "tp", split_axis=0, concat_axis=1, tiled=True)
    held_seqs = arrived.shape[0]
    arranged = arrived.reshape(held_seqs, tp_count, 2, split_at)
    query_all = jnp.transpose(
        arranged[..., :q_width].reshape(held_seqs, tp_count, 2, heads_here, HD), (0, 2, 1, 3, 4)
    ).reshape(held_seqs, 2, HQ, HD)
    key_all = natural_order(arranged[..., q_width : q_width + kv_width], duplicate)
    value_all = natural_order(arranged[..., q_width + kv_width :], duplicate)
    mixed_heads = attend(query_all, key_all, value_all, cache_keys, cache_values, lengths)
    gathered_heads = lax.all_gather(
        mixed_heads.reshape(held_seqs * 2, HQ * HD), "tp", axis=0, tiled=True
    )
    result = lax.dot_general(
        gathered_heads, output_local, (((1,), (1,)), ((), ())), preferred_element_type=jnp.float32
    )
    return result.astype(jnp.bfloat16).reshape(seq_count, 2, -1)


def solution(mesh):
    in_specs = (
        P(("rep", "tp"), None),
        P(("rep", "tp"), None),
        P(("rep", "tp"), None),
        P(("rep", "tp"), None),
        P(),
        P(),
        P("rep", None, None),
        P("rep"),
        P(("rep", "tp"), None, None, None),
        P(("rep", "tp"), None, None, None),
        P(("rep", "tp")),
    )
    out_specs = P("rep", None, "tp")
    return jax.shard_map(body, mesh=mesh, in_specs=in_specs, out_specs=out_specs, check_vma=False)
```

```python
import jax
import jax.numpy as jnp
from jax import lax
from jax.experimental import pallas as pl
from jax.experimental.pallas import tpu as pltpu
from jax.sharding import PartitionSpec as P

D = 8192
HQ = 32
KVH = 4
HD = 128
LMAX = 256
REP = 8
TP = 16
ROWS = D // (REP * TP)
SEQS = 20
TOKENS = 2 * SEQS
ALL_ROWS = TP * TOKENS
MAIN = 32
TAIL = TOKENS - MAIN
Q_ROWS = SEQS * 16
ROPE_THETA = 1000000.0
MESH = pl.DeviceIdType.MESH
BF = jnp.bfloat16
F32 = jnp.float32


def iota(shape, dim):
    return lax.broadcasted_iota(jnp.int32, shape, dim)


def swap_halves(x):
    return pltpu.roll(x, HD // 2, 1)


def top_half(view):
    return view.at[pl.ds(0, view.shape[0] // 2)]


def bottom_half(view):
    return view.at[pl.ds(view.shape[0] // 2, view.shape[0] // 2)]


def left_half(view):
    return view.at[:, pl.ds(0, view.shape[1] // 2)]


def right_half(view):
    return view.at[:, pl.ds(view.shape[1] // 2, view.shape[1] // 2)]


BY_ROWS = (lambda view: view, top_half, bottom_half)
BY_LANES = (lambda view: view, left_half, right_half)


class Gather:
    ARRIVES = (
        ("x", 0), ("m", 0), ("p", 0), ("xm", 0), ("xp", 0),
        ("2", 1), ("2", 2), ("x2", 1), ("x2", 2),
    )
    SENT = (
        ("own", 0, "x"), ("own", 0, "p"), ("own", 0, "m"), ("x", 0, "p"), ("x", 0, "m"),
        ("m", 1, "p"), ("p", 2, "m"), ("2", 1, "x"), ("2", 2, "x"),
    )

    def __init__(self, buffers, parts, blocks, neighbours, send_sems, recv_sems):
        self.buffers = buffers
        self.parts = parts
        self.blocks = blocks
        self.neighbours = neighbours
        self.send_sems = send_sems
        self.recv_sems = recv_sems

    def copies(self, step, arriving):
        if arriving:
            name, part = self.ARRIVES[step]
            device = self.neighbours["x"]
        else:
            name, part, to = self.SENT[step]
            device = self.neighbours[to]
        for b, (buffer, parts) in enumerate(zip(self.buffers, self.parts)):
            view = parts[part](buffer.at[self.blocks[name]])
            yield pltpu.make_async_remote_copy(
                src_ref=view,
                dst_ref=view,
                send_sem=self.send_sems.at[b, step],
                recv_sem=self.recv_sems.at[b, step],
                device_id=device,
                device_id_type=MESH,
            )

    def send(self, *steps):
        for step in steps:
            for copy in self.copies(step, False):
                copy.start()

    def arrive(self, *steps):
        for step in steps:
            for copy in self.copies(step, True):
                copy.wait_recv()

    def finish(self):
        for step in range(9):
            for copy in self.copies(step, False):
                copy.wait_send()


def kernel(
    wq_ref, wk_ref, wv_ref, wo_ref, qa_ref, ka_ref, hid_ref, pos_ref, ck_ref, cv_ref, len_ref,
    out_ref,
    qf, kvf, wq, kvw, wo, hid, stage, ck, cv, outgoing, incoming, att, tail, tail_f32,
    acc, cosine, sine, pick, unpick, q_g, scores, probs, mixed,
    stage_sems, cache_sems, a_send, a_recv, w_send, w_recv, qkv_send, qkv_recv,
    gq_send, gq_recv, go_send, go_recv, ga_send, ga_recv, core_send, core_recv,
):
    r = lax.axis_index("rep")
    t = lax.axis_index("tp")

    x_rep = lax.rem(r + 4, 8)
    base = r // 4 * 4
    other = 4 - base
    z = lax.rem(r, 4)
    zp, zm, z2 = lax.rem(z + 1, 4), lax.rem(z + 3, 4), lax.rem(z + 2, 4)
    rep_blocks = {
        "own": r, "x": x_rep, "p": base + zp, "m": base + zm, "2": base + z2,
        "xp": other + zp, "xm": other + zm, "x2": other + z2,
    }
    rep_neighbours = {"x": (x_rep, t), "p": (base + zp, t), "m": (base + zm, t)}
    y = t // 4
    low = lax.rem(t, 4)
    far = lax.rem(low + 2, 4)
    yp, ym, y2 = lax.rem(y + 1, 4) * 4, lax.rem(y + 3, 4) * 4, lax.rem(y + 2, 4) * 4
    tp_blocks = {
        "own": t, "x": y * 4 + far, "p": yp + low, "m": ym + low, "2": y2 + low,
        "xp": yp + far, "xm": ym + far, "x2": y2 + far,
    }
    tp_neighbours = {k: (r, tp_blocks[k]) for k in ("x", "p", "m")}
    core = t + 1 - 2 * lax.rem(t, 2)
    wo_to = (lax.rem(t, 8), 2 * r + t // 8)
    wo_from = (t // 2, r + 8 * lax.rem(t, 2))
    wo_stays = jnp.logical_and(wo_to[0] == r, wo_to[1] == t)

    barrier = pltpu.get_barrier_semaphore()

    def greet(device):
        pl.semaphore_signal(barrier, inc=1, device_id=device, device_id_type=MESH)

    for k in range(1, TP):
        greet((r, lax.rem(t + k, TP)))
    for device in rep_neighbours.values():
        greet(device)

    @pl.when(jnp.logical_not(wo_stays))
    def _():
        greet(wo_from)

    def hidden_copy(i, slot):
        return pltpu.make_async_copy(
            hid_ref.at[:, :, pl.ds(i * 1024, 1024)], stage.at[slot], stage_sems.at[slot]
        )

    hidden_copy(0, 0).start()
    hidden_copy(1, 1).start()

    factors = []
    for g in range(KVH):
        query_peak = jnp.broadcast_to(
            jnp.max(qa_ref[8 * g : 8 * g + 8, :], axis=0, keepdims=True), (8, HD)
        )
        query_peak = jnp.maximum(query_peak, swap_halves(query_peak))
        key_peak = jnp.broadcast_to(ka_ref[g : g + 1, :], (8, HD))
        key_peak = jnp.maximum(key_peak, swap_halves(key_peak))
        factors.append(jnp.sqrt(key_peak / query_peak)[0:1, :])
    for dst in range(TP):
        factor = jnp.concatenate([factors[dst // 4]] * 2, axis=1)
        qf[dst] = (wq_ref[:, 256 * dst : 256 * dst + 256].astype(F32) * factor).astype(BF)
    for g in range(KVH):
        kvf[g] = (wk_ref[:, HD * g : HD * g + HD].astype(F32) / factors[g]).astype(BF)
        kvf[KVH + g] = wv_ref[:, HD * g : HD * g + HD]

    pl.semaphore_wait(barrier, TP - 1 + 3 + 1 - wo_stays.astype(jnp.int32))

    half = t // 8
    q_rows = pl.ds(pl.multiple_of(t * ROWS, ROWS), ROWS)
    kv_rows = pl.ds(pl.multiple_of(lax.rem(t, 8) * ROWS, ROWS), ROWS)

    def deliver(k, carry):
        dst = lax.rem(t + k, TP)
        pltpu.make_async_remote_copy(
            src_ref=qf.at[dst], dst_ref=wq.at[r, q_rows],
            send_sem=a_send.at[0], recv_sem=a_recv.at[0],
            device_id=(r, dst), device_id_type=MESH,
        ).start()

        @pl.when(lax.rem(dst, 2) == half)
        def _():
            pltpu.make_async_remote_copy(
                src_ref=kvf.at[lax.rem(dst, 4) // 2 * 4 + dst // 4], dst_ref=kvw.at[r, kv_rows],
                send_sem=a_send.at[1], recv_sem=a_recv.at[1],
                device_id=(r, dst), device_id_type=MESH,
            ).start()

        return carry

    lax.fori_loop(1, TP, deliver, 0)
    pltpu.make_async_copy(qf.at[t], wq.at[r, q_rows], a_recv.at[0]).start()
    own_kv = lax.rem(t, 2) == half

    @pl.when(own_kv)
    def _():
        pltpu.make_async_copy(
            kvf.at[lax.rem(t, 4) // 2 * 4 + t // 4], kvw.at[r, kv_rows], a_recv.at[1]
        ).start()

    def wo_copy():
        return pltpu.make_async_remote_copy(
            src_ref=wo_ref, dst_ref=wo.at[wo_to[0]],
            send_sem=w_send, recv_sem=w_recv, device_id=wo_to, device_id_type=MESH,
        )

    @pl.when(jnp.logical_not(wo_stays))
    def _():
        wo_copy().start()

    @pl.when(wo_stays)
    def _():
        pltpu.make_async_copy(wo_ref, wo.at[r], w_recv).start()

    cache_copies = [
        pltpu.make_async_copy(ck_ref, ck, cache_sems.at[0]),
        pltpu.make_async_copy(cv_ref, cv, cache_sems.at[1]),
    ]

    def relayout(i, carry):
        slot = lax.rem(i, 2)
        hidden_copy(i, slot).wait()
        columns = pl.ds(pl.multiple_of(i * 1024, 1024), 1024)
        hid[:, columns] = stage[slot].reshape(ALL_ROWS, 1024)

        @pl.when(i < 6)
        def _():
            hidden_copy(i + 2, slot).start()

        return carry

    lax.fori_loop(0, 8, relayout, 0)

    gather_q = Gather(
        [wq, kvw], [BY_ROWS, BY_ROWS], rep_blocks, rep_neighbours, gq_send, gq_recv
    )
    gather_o = Gather([wo], [BY_ROWS], rep_blocks, rep_neighbours, go_send, go_recv)
    pltpu.make_async_copy(wq.at[r], wq.at[r], a_recv.at[0]).wait()
    pltpu.make_async_copy(kvw.at[r], kvw.at[r], a_recv.at[1]).wait()
    gather_q.send(0, 1, 2)
    for copy in cache_copies:
        copy.start()

    place = jnp.sum(
        jnp.where(
            iota((ALL_ROWS, 320), 0) // 2 == iota((ALL_ROWS, 320), 1),
            pos_ref[...].astype(F32),
            0.0,
        ),
        axis=1,
        keepdims=True,
    ) + lax.rem(iota((ALL_ROWS, 1), 0), 2).astype(F32)
    channel = lax.rem(iota((1, HD), 1), HD // 2).astype(F32)
    angle = place * (ROPE_THETA ** (-2.0 * channel / HD))
    cosine[...] = jnp.cos(angle)
    sine[...] = jnp.sin(angle) * jnp.where(iota((1, HD), 1) < HD // 2, -1.0, 1.0)

    row, col = iota((576, 512), 0), iota((576, 512), 1)
    b, w = row // 16, lax.rem(row, 16)
    source = w // 4 * 128 + lax.rem(w, 2) * TOKENS + 2 * b + lax.rem(w // 2, 2)
    token = lax.rem(row - Q_ROWS + 128, 128)
    col_row, col_dev = lax.rem(col, 128), col // 128
    fresh_row = jnp.logical_and(col_row == 80 + token, token < TOKENS)
    is_key, is_value = row < Q_ROWS + 128, col_dev >= 2
    hit = jnp.where(
        row < Q_ROWS, (col == source).astype(F32),
        jnp.logical_and(fresh_row, is_key != is_value).astype(F32),
    )
    pick[...] = hit.astype(BF)
    row, col = iota((Q_ROWS, 384), 0), iota((Q_ROWS, 384), 1)
    head, token = row // TOKENS, lax.rem(row, TOKENS)
    source = token // 2 * 16 + head // 2 * 4 + lax.rem(token, 2) * 2 + lax.rem(head, 2)
    unpick[...] = (col == source).astype(F32).astype(BF)

    kv_half = lax.rem(t, 2) * 512

    def project(name, first=False):
        block = rep_blocks[name]
        q_at = pl.multiple_of(block * 1024, 1024)
        kv_at = pl.multiple_of(block * 1024 + kv_half, 512)
        for m in range(0, ALL_ROWS, 128):
            q = jnp.dot(hid[m : m + 128, pl.ds(q_at, 1024)], wq[block], preferred_element_type=F32)
            kv = jnp.dot(hid[m : m + 128, pl.ds(kv_at, 512)], kvw[block], preferred_element_type=F32)
            if first:
                acc[m : m + 128, 0:256] = q
                acc[m : m + 128, 256:384] = kv
            else:
                acc[m : m + 128, 0:256] += q
                acc[m : m + 128, 256:384] += kv

    project("own", True)
    gather_q.arrive(1)
    gather_q.send(5)
    gather_q.arrive(2)
    gather_q.send(6)
    gather_q.arrive(0)
    gather_q.send(3, 4)
    project("m")
    project("p")
    project("x")
    gather_q.arrive(5)
    gather_q.send(7)
    gather_q.arrive(6)
    gather_q.send(8)
    pltpu.make_async_copy(wo.at[r], wo.at[r], w_recv).wait()
    gather_o.send(0, 1, 2)
    project("2")
    gather_q.arrive(3)
    project("xm")
    gather_q.arrive(4)
    project("xp")
    gather_q.arrive(7, 8)
    project("x2")

    is_value_device = lax.rem(t // 2, 2) == 1

    def spread(k, carry):
        dst = lax.rem(t + k, TP)
        rows = pl.ds(pl.multiple_of(dst * TOKENS, 8), TOKENS)
        c, s = cosine[rows, :], sine[rows, :]
        q0, q1, kv = acc[rows, 0:128], acc[rows, 128:256], acc[rows, 256:384]
        q0 = q0 * c + swap_halves(q0) * s
        q1 = q1 * c + swap_halves(q1) * s
        kv = jnp.where(is_value_device, kv, kv * c + swap_halves(kv) * s)
        packed = jnp.concatenate([q0, q1, kv, jnp.zeros((8, HD), F32)], axis=0).astype(BF)

        outgoing[dst] = packed

        @pl.when(k < TP)
        def _():
            pltpu.make_async_remote_copy(
                src_ref=outgoing.at[dst], dst_ref=incoming.at[t],
                send_sem=qkv_send, recv_sem=qkv_recv,
                device_id=(r, dst), device_id_type=MESH,
            ).start()

        @pl.when(k == TP)
        def _():
            pltpu.make_async_copy(outgoing.at[dst], incoming.at[t], qkv_recv).start()

        return carry

    lax.fori_loop(1, TP + 1, spread, 0)
    gather_o.arrive(1)
    gather_o.send(5)
    gather_o.arrive(2)
    gather_o.send(6)
    gather_o.arrive(0)
    gather_o.send(3, 4)

    for copy in cache_copies:
        copy.wait()
    pltpu.make_async_copy(incoming, incoming, qkv_recv).wait()

    lengths = jnp.sum(
        jnp.where(
            iota((Q_ROWS, SEQS), 0) // 16 == iota((Q_ROWS, SEQS), 1), len_ref[...].astype(F32), 0.0
        ),
        axis=1,
        keepdims=True,
    )
    live = iota((Q_ROWS, LMAX), 1).astype(F32) < lengths
    row, col = iota((Q_ROWS, 128), 0), iota((Q_ROWS, 128), 1)
    fresh_live = jnp.logical_and(
        row // 16 == col // 2, lax.rem(col, 2) <= lax.rem(lax.rem(row, 16) // 2, 2)
    )
    mixed[Q_ROWS:384, :] = jnp.zeros((384 - Q_ROWS, HD), BF)

    def attend(g, carry):
        gathered = incoming[pl.ds(g * 4, 4)].reshape(512, HD)
        ordered = jnp.dot(pick[...], gathered, preferred_element_type=F32).astype(BF)
        q_g[...] = ordered[0:Q_ROWS]
        key_new, value_new = ordered[Q_ROWS : Q_ROWS + 128], ordered[Q_ROWS + 128 :]
        for b in range(SEQS):
            scores[16 * b : 16 * b + 16, :] = lax.dot_general(
                q_g[16 * b : 16 * b + 16, :], ck[b, g], (((1,), (1,)), ((), ())),
                preferred_element_type=F32,
            )
        scale = HD ** (-0.5)
        cached = jnp.where(live, scores[...] * scale, -jnp.inf)
        fresh = lax.dot_general(
            q_g[...], key_new, (((1,), (1,)), ((), ())), preferred_element_type=F32
        )
        fresh = jnp.where(fresh_live, fresh * scale, -jnp.inf)
        top = jnp.maximum(
            jnp.max(cached, axis=1, keepdims=True), jnp.max(fresh, axis=1, keepdims=True)
        )
        cached = jnp.exp(cached - top)
        fresh = jnp.exp(fresh - top)
        total = jnp.sum(cached, axis=1, keepdims=True) + jnp.sum(fresh, axis=1, keepdims=True)
        probs[...] = cached.astype(BF)
        fresh_part = jnp.dot(fresh.astype(BF), value_new, preferred_element_type=F32)
        parts = [
            jnp.dot(probs[16 * b : 16 * b + 16, :], cv[b, g], preferred_element_type=F32)
            for b in range(SEQS)
        ]
        mixed[0:Q_ROWS, :] = (
            (jnp.concatenate(parts, axis=0) + fresh_part) / total
        ).astype(BF)
        by_head = jnp.dot(unpick[...], mixed[...], preferred_element_type=F32)
        lanes = pl.multiple_of(g * 1024, 1024)
        tail_lanes = pl.multiple_of(lax.rem(g, 2) * 1024, 1024)
        tail_rows = pl.multiple_of(g // 2 * 8, 8)
        heads = [by_head[TOKENS * h : TOKENS * h + TOKENS] for h in range(8)]
        att[t, :, pl.ds(lanes, 1024)] = jnp.concatenate([x[:MAIN] for x in heads], axis=1).astype(BF)
        tail_f32[pl.ds(tail_rows, 8), pl.ds(tail_lanes, 1024)] = jnp.concatenate(
            [x[MAIN:] for x in heads], axis=1
        )
        return carry

    lax.fori_loop(0, KVH, attend, 0)
    tail[t] = tail_f32[...].astype(BF)

    gather_a = Gather(
        [att, tail], [BY_ROWS, BY_LANES], tp_blocks, tp_neighbours, ga_send, ga_recv
    )
    names = ("own", "m", "p", "x", "2", "xm", "xp", "x2")

    def to_core(i, block, start):
        for b, buffer in enumerate((att, tail)):
            copy = pltpu.make_async_remote_copy(
                src_ref=buffer.at[block], dst_ref=buffer.at[block],
                send_sem=core_send.at[b, i], recv_sem=core_recv.at[b, i],
                device_id=(r, core), device_id_type=MESH,
            )
            if start == 0:
                copy.start()
            elif start == 1:
                copy.wait_recv()
            else:
                copy.wait_send()

    def share(name):
        to_core(names.index(name), tp_blocks[name], 0)

    gather_a.send(0, 1, 2)
    share("own")
    gather_o.arrive(5)
    gather_o.send(7)
    gather_o.arrive(6)
    gather_o.send(8)
    gather_a.arrive(1)
    gather_a.send(5)
    gather_a.arrive(2)
    gather_a.send(6)
    gather_a.arrive(0)
    gather_a.send(3, 4)
    share("m")
    share("p")
    share("x")
    gather_a.arrive(5)
    gather_a.send(7)
    gather_a.arrive(6)
    gather_a.send(8)
    share("2")
    gather_a.arrive(3)
    share("xm")
    gather_a.arrive(4)
    share("xp")
    gather_a.arrive(7, 8)
    share("x2")
    gather_o.arrive(3, 4, 7, 8)
    flip = 1 - 2 * lax.rem(t, 2)
    for i, name in enumerate(names):
        to_core(i, tp_blocks[name] + flip, 1)

    def output(i, carry):
        main = att[pl.ds(i * 4, 4)].reshape(4 * MAIN, HQ * HD)
        last = tail[pl.ds(i * 4, 4)].reshape(64, HQ * HD // 2)
        full = wo[...].reshape(512, HQ * HD)
        dims = (((1,), (1,)), ((), ()))
        main = lax.dot_general(main, full, dims, preferred_element_type=F32)
        first = lax.dot_general(last, full[:, : HQ * HD // 2], dims, preferred_element_type=F32)
        second = lax.dot_general(last, full[:, HQ * HD // 2 :], dims, preferred_element_type=F32)
        rows = []
        for s in range(4):
            rows.append(main[MAIN * s : MAIN * s + MAIN])
            rows.append(first[16 * s : 16 * s + 8] + second[16 * s + 8 : 16 * s + 16])
        at = pl.ds(pl.multiple_of(i * 160, 160), 160)
        out_ref[at, :] = jnp.concatenate(rows, axis=0).astype(BF)
        return carry

    lax.fori_loop(0, 4, output, 0)

    def sent_q(k, carry):
        dst = lax.rem(t + k, TP)
        pltpu.make_async_copy(qf.at[dst], qf.at[dst], a_send.at[0]).wait()
        pltpu.make_async_copy(outgoing.at[dst], outgoing.at[dst], qkv_send).wait()

        @pl.when(lax.rem(dst, 2) == half)
        def _():
            pltpu.make_async_copy(kvf.at[0], kvf.at[0], a_send.at[1]).wait()

        return carry

    lax.fori_loop(1, TP, sent_q, 0)

    @pl.when(jnp.logical_not(wo_stays))
    def _():
        wo_copy().wait_send()

    gather_q.finish()
    gather_o.finish()
    gather_a.finish()
    for i, name in enumerate(names):
        to_core(i, tp_blocks[name], 2)


def body(
    query_weight, key_weight, value_weight, output_weight, query_amax, key_amax,
    hidden, positions, cache_keys, cache_values, lengths,
):
    vmem = pl.BlockSpec(memory_space=pltpu.VMEM)
    hbm = pl.BlockSpec(memory_space=pl.ANY)
    dma = pltpu.SemaphoreType.DMA
    result = pl.pallas_call(
        kernel,
        out_shape=jax.ShapeDtypeStruct((ALL_ROWS, 512), BF),
        in_specs=[vmem, vmem, vmem, hbm, vmem, vmem, hbm, vmem, hbm, hbm, vmem],
        out_specs=vmem,
        scratch_shapes=[
            pltpu.VMEM((TP, ROWS, 256), BF),
            pltpu.VMEM((2 * KVH, ROWS, HD), BF),
            pltpu.VMEM((REP, TP * ROWS, 256), BF),
            pltpu.VMEM((REP, 8 * ROWS, HD), BF),
            pltpu.VMEM((REP, ROWS, HQ * HD), BF),
            pltpu.VMEM((ALL_ROWS, D), BF),
            pltpu.VMEM((2, 320, 2, 1024), BF),
            pltpu.VMEM((SEQS, KVH, LMAX, HD), BF),
            pltpu.VMEM((SEQS, KVH, LMAX, HD), BF),
            pltpu.VMEM((TP, 128, HD), BF),
            pltpu.VMEM((TP, 128, HD), BF),
            pltpu.VMEM((TP, MAIN, HQ * HD), BF),
            pltpu.VMEM((TP, 2 * TAIL, HQ * HD // 2), BF),
            pltpu.VMEM((2 * TAIL, HQ * HD // 2), F32),
            pltpu.VMEM((ALL_ROWS, 384), F32),
            pltpu.VMEM((ALL_ROWS, HD), F32),
            pltpu.VMEM((ALL_ROWS, HD), F32),
            pltpu.VMEM((576, 512), BF),
            pltpu.VMEM((Q_ROWS, 384), BF),
            pltpu.VMEM((Q_ROWS, HD), BF),
            pltpu.VMEM((Q_ROWS, LMAX), F32),
            pltpu.VMEM((Q_ROWS, LMAX), BF),
            pltpu.VMEM((384, HD), BF),
            dma((2,)), dma((2,)), dma((2,)), dma((2,)), dma, dma, dma, dma,
            dma((2, 9)), dma((2, 9)), dma((1, 9)), dma((1, 9)), dma((2, 9)), dma((2, 9)),
            dma((2, 8)), dma((2, 8)),
        ],
        compiler_params=pltpu.CompilerParams(
            collective_id=0, has_side_effects=True, vmem_limit_bytes=62 * 2**20
        ),
    )(
        query_weight, key_weight, value_weight, output_weight,
        query_amax.reshape(HQ, HD), key_amax.reshape(KVH, HD),
        hidden, positions.reshape(1, -1), cache_keys, cache_values, lengths.reshape(1, -1),
    )
    return result.reshape(hidden.shape[0], 2, 512)


def solution(mesh):
    in_specs = (
        P(("rep", "tp"), None),
        P(("rep", "tp"), None),
        P(("rep", "tp"), None),
        P(("rep", "tp"), None),
        P(),
        P(),
        P("rep", None, None),
        P("rep"),
        P(("rep", "tp"), None, None, None),
        P(("rep", "tp"), None, None, None),
        P(("rep", "tp")),
    )
    out_specs = P("rep", None, "tp")

    def run(*args):
        with jax.sharding.use_abstract_mesh(mesh.abstract_mesh):
            return jax.shard_map(
                body, mesh=mesh, in_specs=in_specs, out_specs=out_specs, check_vma=False
            )(*args)

    return run
```

```python
import jax
import jax.numpy as jnp
from jax import lax
from jax.experimental import pallas as pl
from jax.experimental.pallas import tpu as pltpu
from jax.sharding import PartitionSpec as P

D = 8192
HQ = 32
KVH = 4
HD = 128
LMAX = 256
REP = 8
TP = 16
ROWS = D // (REP * TP)
SEQS = 20
TOKENS = 2 * SEQS
ALL_ROWS = TP * TOKENS
MAIN = 32
TAIL = TOKENS - MAIN
Q_ROWS = SEQS * 16
ROPE_THETA = 1000000.0
MESH = pl.DeviceIdType.MESH
BF = jnp.bfloat16
F32 = jnp.float32


def iota(shape, dim):
    return lax.broadcasted_iota(jnp.int32, shape, dim)


def swap_halves(x):
    return pltpu.roll(x, HD // 2, 1)


def top_half(view):
    return view.at[pl.ds(0, view.shape[0] // 2)]


def bottom_half(view):
    return view.at[pl.ds(view.shape[0] // 2, view.shape[0] // 2)]


def left_half(view):
    return view.at[:, pl.ds(0, view.shape[1] // 2)]


def right_half(view):
    return view.at[:, pl.ds(view.shape[1] // 2, view.shape[1] // 2)]


BY_ROWS = (lambda view: view, top_half, bottom_half)
BY_LANES = (lambda view: view, left_half, right_half)


class Gather:
    ARRIVES = (
        ("x", 0), ("m", 0), ("p", 0), ("xm", 0), ("xp", 0),
        ("2", 1), ("2", 2), ("x2", 1), ("x2", 2),
    )
    SENT = (
        ("own", 0, "x"), ("own", 0, "p"), ("own", 0, "m"), ("x", 0, "p"), ("x", 0, "m"),
        ("m", 1, "p"), ("p", 2, "m"), ("2", 1, "x"), ("2", 2, "x"),
    )

    def __init__(self, buffers, parts, blocks, neighbours, send_sems, recv_sems):
        self.buffers = buffers
        self.parts = parts
        self.blocks = blocks
        self.neighbours = neighbours
        self.send_sems = send_sems
        self.recv_sems = recv_sems

    def copies(self, step, arriving):
        if arriving:
            name, part = self.ARRIVES[step]
            device = self.neighbours["x"]
        else:
            name, part, to = self.SENT[step]
            device = self.neighbours[to]
        for b, (buffer, parts) in enumerate(zip(self.buffers, self.parts)):
            view = parts[part](buffer.at[self.blocks[name]])
            yield pltpu.make_async_remote_copy(
                src_ref=view,
                dst_ref=view,
                send_sem=self.send_sems.at[b, step],
                recv_sem=self.recv_sems.at[b, step],
                device_id=device,
                device_id_type=MESH,
            )

    def send(self, *steps):
        for step in steps:
            for copy in self.copies(step, False):
                copy.start()

    def arrive(self, *steps):
        for step in steps:
            for copy in self.copies(step, True):
                copy.wait_recv()

    def finish(self):
        for step in range(9):
            for copy in self.copies(step, False):
                copy.wait_send()


def kernel(
    wq_ref, wk_ref, wv_ref, wo_ref, qa_ref, ka_ref, hid_ref, pos_ref, ck_ref, cv_ref, len_ref,
    out_ref,
    qf, kvf, wq, kvw, wo_stage, wo, hid, stage, ck, cv, outgoing, incoming, att, tail, tail_f32,
    acc, cosine, sine, pick, unpick, q_g, scores, probs, mixed, main_out, tail_out,
    stage_sems, cache_sems, a_send, a_recv, w_send, w_recv, qkv_send, qkv_recv,
    gq_send, gq_recv, go_send, go_recv, ga_send, ga_recv, core_send, core_recv,
):
    r = lax.axis_index("rep")
    t = lax.axis_index("tp")

    x_rep = lax.rem(r + 4, 8)
    base = r // 4 * 4
    other = 4 - base
    z = lax.rem(r, 4)
    zp, zm, z2 = lax.rem(z + 1, 4), lax.rem(z + 3, 4), lax.rem(z + 2, 4)
    rep_blocks = {
        "own": r, "x": x_rep, "p": base + zp, "m": base + zm, "2": base + z2,
        "xp": other + zp, "xm": other + zm, "x2": other + z2,
    }
    rep_neighbours = {"x": (x_rep, t), "p": (base + zp, t), "m": (base + zm, t)}
    y = t // 4
    low = lax.rem(t, 4)
    far = lax.rem(low + 2, 4)
    yp, ym, y2 = lax.rem(y + 1, 4) * 4, lax.rem(y + 3, 4) * 4, lax.rem(y + 2, 4) * 4
    tp_blocks = {
        "own": t, "x": y * 4 + far, "p": yp + low, "m": ym + low, "2": y2 + low,
        "xp": yp + far, "xm": ym + far, "x2": y2 + far,
    }
    tp_neighbours = {k: (r, tp_blocks[k]) for k in ("x", "p", "m")}
    core = t + 1 - 2 * lax.rem(t, 2)
    barrier = pltpu.get_barrier_semaphore()

    def greet(device):
        pl.semaphore_signal(barrier, inc=1, device_id=device, device_id_type=MESH)

    for k in range(1, TP):
        greet((r, lax.rem(t + k, TP)))
    for k in range(1, REP):
        greet((lax.rem(r + k, REP), t))

    def hidden_copy(i, slot):
        return pltpu.make_async_copy(
            hid_ref.at[:, :, pl.ds(i * 1024, 1024)], stage.at[slot], stage_sems.at[slot]
        )

    hidden_copy(0, 0).start()
    hidden_copy(1, 1).start()

    factors = []
    for g in range(KVH):
        query_peak = jnp.broadcast_to(
            jnp.max(qa_ref[8 * g : 8 * g + 8, :], axis=0, keepdims=True), (8, HD)
        )
        query_peak = jnp.maximum(query_peak, swap_halves(query_peak))
        key_peak = jnp.broadcast_to(ka_ref[g : g + 1, :], (8, HD))
        key_peak = jnp.maximum(key_peak, swap_halves(key_peak))
        factors.append(jnp.sqrt(key_peak / query_peak)[0:1, :])
    for dst in range(TP):
        factor = jnp.concatenate([factors[dst // 4]] * 2, axis=1)
        qf[dst] = (wq_ref[:, 256 * dst : 256 * dst + 256].astype(F32) * factor).astype(BF)
    for g in range(KVH):
        kvf[g] = (wk_ref[:, HD * g : HD * g + HD].astype(F32) / factors[g]).astype(BF)
        kvf[KVH + g] = wv_ref[:, HD * g : HD * g + HD]

    pl.semaphore_wait(barrier, TP - 1 + REP - 1)

    def wo_columns(i):
        return wo_ref.at[:, pl.ds(pl.multiple_of(i * 512, 512), 512)]

    def wo_scatter(k, carry):
        to = lax.rem(r + k, REP)
        pltpu.make_async_remote_copy(
            src_ref=wo_columns(to), dst_ref=wo_stage.at[r],
            send_sem=w_send.at[0], recv_sem=w_recv.at[0],
            device_id=(to, t), device_id_type=MESH,
        ).start()
        return carry

    lax.fori_loop(1, REP, wo_scatter, 0)
    pltpu.make_async_copy(wo_columns(r), wo_stage.at[r], w_recv.at[0]).start()

    half = t // 8
    q_rows = pl.ds(pl.multiple_of(t * ROWS, ROWS), ROWS)
    kv_rows = pl.ds(pl.multiple_of(lax.rem(t, 8) * ROWS, ROWS), ROWS)

    def deliver(k, carry):
        dst = lax.rem(t + k, TP)
        pltpu.make_async_remote_copy(
            src_ref=qf.at[dst], dst_ref=wq.at[r, q_rows],
            send_sem=a_send.at[0], recv_sem=a_recv.at[0],
            device_id=(r, dst), device_id_type=MESH,
        ).start()

        @pl.when(lax.rem(dst, 2) == half)
        def _():
            pltpu.make_async_remote_copy(
                src_ref=kvf.at[lax.rem(dst, 4) // 2 * 4 + dst // 4], dst_ref=kvw.at[r, kv_rows],
                send_sem=a_send.at[1], recv_sem=a_recv.at[1],
                device_id=(r, dst), device_id_type=MESH,
            ).start()

        return carry

    lax.fori_loop(1, TP, deliver, 0)
    pltpu.make_async_copy(qf.at[t], wq.at[r, q_rows], a_recv.at[0]).start()
    own_kv = lax.rem(t, 2) == half

    @pl.when(own_kv)
    def _():
        pltpu.make_async_copy(
            kvf.at[lax.rem(t, 4) // 2 * 4 + t // 4], kvw.at[r, kv_rows], a_recv.at[1]
        ).start()

    wo_rows = pl.ds(pl.multiple_of(lax.rem(t, 8) * ROWS, ROWS), ROWS)

    def wo_deliver(i, carry):
        dst = 2 * i + half

        @pl.when(dst != t)
        def _():
            pltpu.make_async_remote_copy(
                src_ref=wo_stage.at[i], dst_ref=wo.at[r, wo_rows],
                send_sem=w_send.at[1], recv_sem=w_recv.at[1],
                device_id=(r, dst), device_id_type=MESH,
            ).start()

        @pl.when(dst == t)
        def _():
            pltpu.make_async_copy(wo_stage.at[i], wo.at[r, wo_rows], w_recv.at[1]).start()

        return carry

    cache_copies = [
        pltpu.make_async_copy(ck_ref, ck, cache_sems.at[0]),
        pltpu.make_async_copy(cv_ref, cv, cache_sems.at[1]),
    ]

    def relayout(i, carry):
        slot = lax.rem(i, 2)
        hidden_copy(i, slot).wait()
        columns = pl.ds(pl.multiple_of(i * 1024, 1024), 1024)
        hid[:, columns] = stage[slot].reshape(ALL_ROWS, 1024)

        @pl.when(i < 6)
        def _():
            hidden_copy(i + 2, slot).start()

        return carry

    gather_q = Gather(
        [wq, kvw], [BY_ROWS, BY_ROWS], rep_blocks, rep_neighbours, gq_send, gq_recv
    )
    gather_o = Gather([wo], [BY_ROWS], rep_blocks, rep_neighbours, go_send, go_recv)
    pltpu.make_async_copy(wq.at[r], wq.at[r], a_recv.at[0]).wait()
    pltpu.make_async_copy(kvw.at[r], kvw.at[r], a_recv.at[1]).wait()
    gather_q.send(0, 1, 2)
    pltpu.make_async_copy(wo_stage, wo_stage, w_recv.at[0]).wait()
    lax.fori_loop(0, REP, wo_deliver, 0)
    for copy in cache_copies:
        copy.start()
    lax.fori_loop(0, 8, relayout, 0)

    place = jnp.sum(
        jnp.where(
            iota((ALL_ROWS, 320), 0) // 2 == iota((ALL_ROWS, 320), 1),
            pos_ref[...].astype(F32),
            0.0,
        ),
        axis=1,
        keepdims=True,
    ) + lax.rem(iota((ALL_ROWS, 1), 0), 2).astype(F32)
    channel = lax.rem(iota((1, HD), 1), HD // 2).astype(F32)
    angle = place * (ROPE_THETA ** (-2.0 * channel / HD))
    cosine[...] = jnp.cos(angle)
    sine[...] = jnp.sin(angle) * jnp.where(iota((1, HD), 1) < HD // 2, -1.0, 1.0)

    main_out[...] = jnp.zeros_like(main_out)
    tail_out[...] = jnp.zeros_like(tail_out)

    row, col = iota((576, 512), 0), iota((576, 512), 1)
    b, w = row // 16, lax.rem(row, 16)
    source = w // 4 * 128 + lax.rem(w, 2) * TOKENS + 2 * b + lax.rem(w // 2, 2)
    token = lax.rem(row - Q_ROWS + 128, 128)
    col_row, col_dev = lax.rem(col, 128), col // 128
    fresh_row = jnp.logical_and(col_row == 80 + token, token < TOKENS)
    is_key, is_value = row < Q_ROWS + 128, col_dev >= 2
    hit = jnp.where(
        row < Q_ROWS, (col == source).astype(F32),
        jnp.logical_and(fresh_row, is_key != is_value).astype(F32),
    )
    pick[...] = hit.astype(BF)
    row, col = iota((Q_ROWS, 384), 0), iota((Q_ROWS, 384), 1)
    head, token = row // TOKENS, lax.rem(row, TOKENS)
    source = token // 2 * 16 + head // 2 * 4 + lax.rem(token, 2) * 2 + lax.rem(head, 2)
    unpick[...] = (col == source).astype(F32).astype(BF)

    kv_half = lax.rem(t, 2) * 512

    def project(name, first=False):
        block = rep_blocks[name]
        q_at = pl.multiple_of(block * 1024, 1024)
        kv_at = pl.multiple_of(block * 1024 + kv_half, 512)
        for m in range(0, ALL_ROWS, 128):
            q = jnp.dot(hid[m : m + 128, pl.ds(q_at, 1024)], wq[block], preferred_element_type=F32)
            kv = jnp.dot(hid[m : m + 128, pl.ds(kv_at, 512)], kvw[block], preferred_element_type=F32)
            if first:
                acc[m : m + 128, 0:256] = q
                acc[m : m + 128, 256:384] = kv
            else:
                acc[m : m + 128, 0:256] += q
                acc[m : m + 128, 256:384] += kv

    project("own", True)
    gather_q.arrive(1)
    gather_q.send(5)
    gather_q.arrive(2)
    gather_q.send(6)
    gather_q.arrive(0)
    gather_q.send(3, 4)
    project("m")
    project("p")
    project("x")
    gather_q.arrive(5)
    gather_q.send(7)
    gather_q.arrive(6)
    gather_q.send(8)
    project("2")
    pltpu.make_async_copy(wo.at[r], wo.at[r], w_recv.at[1]).wait()
    gather_q.arrive(3)
    gather_q.arrive(4)
    gather_o.send(1, 2)
    project("xm")
    project("xp")
    gather_q.arrive(7, 8)
    gather_o.send(0)
    project("x2")

    is_value_device = lax.rem(t // 2, 2) == 1

    def spread(k, carry):
        dst = lax.rem(t + k, TP)
        rows = pl.ds(pl.multiple_of(dst * TOKENS, 8), TOKENS)
        c, s = cosine[rows, :], sine[rows, :]
        q0, q1, kv = acc[rows, 0:128], acc[rows, 128:256], acc[rows, 256:384]
        q0 = q0 * c + swap_halves(q0) * s
        q1 = q1 * c + swap_halves(q1) * s
        kv = jnp.where(is_value_device, kv, kv * c + swap_halves(kv) * s)
        packed = jnp.concatenate([q0, q1, kv, jnp.zeros((8, HD), F32)], axis=0).astype(BF)
        outgoing[dst] = packed

        @pl.when(k < TP)
        def _():
            pltpu.make_async_remote_copy(
                src_ref=outgoing.at[dst], dst_ref=incoming.at[t],
                send_sem=qkv_send, recv_sem=qkv_recv,
                device_id=(r, dst), device_id_type=MESH,
            ).start()

        @pl.when(k == TP)
        def _():
            pltpu.make_async_copy(outgoing.at[dst], incoming.at[t], qkv_recv).start()

        return carry

    lax.fori_loop(1, TP + 1, spread, 0)

    for copy in cache_copies:
        copy.wait()
    pltpu.make_async_copy(incoming, incoming, qkv_recv).wait()

    lengths = jnp.sum(
        jnp.where(
            iota((Q_ROWS, SEQS), 0) // 16 == iota((Q_ROWS, SEQS), 1), len_ref[...].astype(F32), 0.0
        ),
        axis=1,
        keepdims=True,
    )
    live = iota((Q_ROWS, LMAX), 1).astype(F32) < lengths
    row, col = iota((Q_ROWS, 128), 0), iota((Q_ROWS, 128), 1)
    fresh_live = jnp.logical_and(
        row // 16 == col // 2, lax.rem(col, 2) <= lax.rem(lax.rem(row, 16) // 2, 2)
    )
    mixed[Q_ROWS:384, :] = jnp.zeros((384 - Q_ROWS, HD), BF)

    def attend(g, carry):
        gathered = incoming[pl.ds(g * 4, 4)].reshape(512, HD)
        ordered = jnp.dot(pick[...], gathered, preferred_element_type=F32).astype(BF)
        q_g[...] = ordered[0:Q_ROWS]
        key_new, value_new = ordered[Q_ROWS : Q_ROWS + 128], ordered[Q_ROWS + 128 :]
        for b in range(SEQS):
            scores[16 * b : 16 * b + 16, :] = lax.dot_general(
                q_g[16 * b : 16 * b + 16, :], ck[b, g], (((1,), (1,)), ((), ())),
                preferred_element_type=F32,
            )
        scale = HD ** (-0.5)
        cached = jnp.where(live, scores[...] * scale, -jnp.inf)
        fresh = lax.dot_general(
            q_g[...], key_new, (((1,), (1,)), ((), ())), preferred_element_type=F32
        )
        fresh = jnp.where(fresh_live, fresh * scale, -jnp.inf)
        top = jnp.maximum(
            jnp.max(cached, axis=1, keepdims=True), jnp.max(fresh, axis=1, keepdims=True)
        )
        cached = jnp.exp(cached - top)
        fresh = jnp.exp(fresh - top)
        total = jnp.sum(cached, axis=1, keepdims=True) + jnp.sum(fresh, axis=1, keepdims=True)
        probs[...] = cached.astype(BF)
        fresh_part = jnp.dot(fresh.astype(BF), value_new, preferred_element_type=F32)
        parts = [
            jnp.dot(probs[16 * b : 16 * b + 16, :], cv[b, g], preferred_element_type=F32)
            for b in range(SEQS)
        ]
        mixed[0:Q_ROWS, :] = (
            (jnp.concatenate(parts, axis=0) + fresh_part) / total
        ).astype(BF)
        by_head = jnp.dot(unpick[...], mixed[...], preferred_element_type=F32)
        lanes = pl.multiple_of(g * 1024, 1024)
        tail_lanes = pl.multiple_of(lax.rem(g, 2) * 1024, 1024)
        tail_rows = pl.multiple_of(g // 2 * 8, 8)
        heads = [by_head[TOKENS * h : TOKENS * h + TOKENS] for h in range(8)]
        att[t, :, pl.ds(lanes, 1024)] = jnp.concatenate([x[:MAIN] for x in heads], axis=1).astype(BF)
        tail_f32[pl.ds(tail_rows, 8), pl.ds(tail_lanes, 1024)] = jnp.concatenate(
            [x[MAIN:] for x in heads], axis=1
        )
        return carry

    lax.fori_loop(0, 2, attend, 0)
    gather_o.arrive(1)
    gather_o.send(5)
    gather_o.arrive(2)
    gather_o.send(6)
    gather_o.arrive(0)
    gather_o.send(3, 4)
    lax.fori_loop(2, KVH, attend, 0)
    tail[t] = tail_f32[...].astype(BF)

    gather_a = Gather(
        [att, tail], [BY_ROWS, BY_LANES], tp_blocks, tp_neighbours, ga_send, ga_recv
    )
    names = ("own", "m", "p", "x", "2", "xm", "xp", "x2")

    def to_core(i, block, start):
        for b, buffer in enumerate((att, tail)):
            copy = pltpu.make_async_remote_copy(
                src_ref=buffer.at[block], dst_ref=buffer.at[block],
                send_sem=core_send.at[b, i], recv_sem=core_recv.at[b, i],
                device_id=(r, core), device_id_type=MESH,
            )
            if start == 0:
                copy.start()
            elif start == 1:
                copy.wait_recv()
            else:
                copy.wait_send()

    def share(name):
        to_core(names.index(name), tp_blocks[name], 0)

    gather_a.send(0, 1, 2)
    share("own")
    gather_a.arrive(1)
    gather_a.send(5)
    gather_a.arrive(2)
    gather_a.send(6)
    gather_a.arrive(0)
    gather_a.send(3, 4)
    share("m")
    share("p")
    share("x")
    gather_o.arrive(5)
    gather_o.send(7)
    gather_o.arrive(6)
    gather_o.send(8)
    gather_a.arrive(5)
    gather_a.send(7)
    gather_a.arrive(6)
    gather_a.send(8)
    share("2")

    chips = {name: tp_blocks[name] // 2 * 2 for name in names}
    flip = 1 - 2 * lax.rem(t, 2)

    def from_core(*group):
        for name in group:
            to_core(names.index(name), tp_blocks[name] + flip, 1)

    def output(i, group, chunks):
        for chunk in chunks:
            block = rep_blocks[chunk]
            lanes = pl.ds(pl.multiple_of(block * 512, 512), 512)
            tail_lanes = pl.ds(pl.multiple_of(lax.rem(block, 4) * 512, 512), 512)
            rows = [att[pl.ds(chips[name], 2), :, lanes].reshape(2 * MAIN, 512) for name in group]
            rows += [
                tail[pl.ds(chips[name], 2), :, tail_lanes].reshape(4 * TAIL, 512) for name in group
            ]
            product = lax.dot_general(
                jnp.concatenate(rows, axis=0), wo[block], (((1,), (1,)), ((), ())),
                preferred_element_type=F32,
            )
            main_out[i] += product[:256]
            tail_out[i, block // 4] += product[256:]

    def store(i, group):
        for n, name in enumerate(group):
            rows = []
            for s in (2 * n, 2 * n + 1):
                rows.append(main_out[i, MAIN * s : MAIN * s + MAIN, :])
                rows.append(
                    tail_out[i, 0, 16 * s : 16 * s + 8, :]
                    + tail_out[i, 1, 16 * s + 8 : 16 * s + 16, :]
                )
            at = pl.ds(pl.multiple_of(chips[name] * TOKENS, 2 * TOKENS), 2 * TOKENS)
            out_ref[at, :] = jnp.concatenate(rows, axis=0).astype(BF)

    near, distant = ("own", "m", "p", "x"), ("2", "xm", "xp", "x2")
    from_core(*near)
    output(0, near, ("own", "m", "p", "x", "2"))
    gather_a.arrive(3)
    share("xm")
    gather_a.arrive(4)
    share("xp")
    gather_o.arrive(3, 4, 7, 8)
    output(0, near, ("xm", "xp", "x2"))
    gather_a.arrive(7, 8)
    share("x2")
    store(0, near)
    from_core(*distant)
    output(1, distant, ("own", "m", "p", "x") + distant)
    store(1, distant)

    def sent_q(k, carry):
        dst = lax.rem(t + k, TP)
        pltpu.make_async_copy(qf.at[dst], qf.at[dst], a_send.at[0]).wait()
        pltpu.make_async_copy(outgoing.at[dst], outgoing.at[dst], qkv_send).wait()

        @pl.when(lax.rem(dst, 2) == half)
        def _():
            pltpu.make_async_copy(kvf.at[0], kvf.at[0], a_send.at[1]).wait()

        return carry

    lax.fori_loop(1, TP, sent_q, 0)

    def sent_o(i, carry):
        pltpu.make_async_copy(wo_stage.at[i], wo_stage.at[i], w_send.at[0]).wait()
        return carry

    lax.fori_loop(1, REP, sent_o, 0)

    def delivered_o(i, carry):
        @pl.when(2 * i + half != t)
        def _():
            pltpu.make_async_copy(wo_stage.at[i], wo_stage.at[i], w_send.at[1]).wait()

        return carry

    lax.fori_loop(0, REP, delivered_o, 0)
    gather_q.finish()
    gather_o.finish()
    gather_a.finish()
    for i, name in enumerate(names):
        to_core(i, tp_blocks[name], 2)


def body(
    query_weight, key_weight, value_weight, output_weight, query_amax, key_amax,
    hidden, positions, cache_keys, cache_values, lengths,
):
    vmem = pl.BlockSpec(memory_space=pltpu.VMEM)
    hbm = pl.BlockSpec(memory_space=pl.ANY)
    dma = pltpu.SemaphoreType.DMA
    result = pl.pallas_call(
        kernel,
        out_shape=jax.ShapeDtypeStruct((ALL_ROWS, 512), BF),
        in_specs=[vmem, vmem, vmem, hbm, vmem, vmem, hbm, vmem, hbm, hbm, vmem],
        out_specs=vmem,
        scratch_shapes=[
            pltpu.VMEM((TP, ROWS, 256), BF),
            pltpu.VMEM((2 * KVH, ROWS, HD), BF),
            pltpu.VMEM((REP, TP * ROWS, 256), BF),
            pltpu.VMEM((REP, 8 * ROWS, HD), BF),
            pltpu.VMEM((REP, ROWS, 512), BF),
            pltpu.VMEM((REP, 512, 512), BF),
            pltpu.VMEM((ALL_ROWS, D), BF),
            pltpu.VMEM((2, 320, 2, 1024), BF),
            pltpu.VMEM((SEQS, KVH, LMAX, HD), BF),
            pltpu.VMEM((SEQS, KVH, LMAX, HD), BF),
            pltpu.VMEM((TP, 128, HD), BF),
            pltpu.VMEM((TP, 128, HD), BF),
            pltpu.VMEM((TP, MAIN, HQ * HD), BF),
            pltpu.VMEM((TP, 2 * TAIL, HQ * HD // 2), BF),
            pltpu.VMEM((2 * TAIL, HQ * HD // 2), F32),
            pltpu.VMEM((ALL_ROWS, 384), F32),
            pltpu.VMEM((ALL_ROWS, HD), F32),
            pltpu.VMEM((ALL_ROWS, HD), F32),
            pltpu.VMEM((576, 512), BF),
            pltpu.VMEM((Q_ROWS, 384), BF),
            pltpu.VMEM((Q_ROWS, HD), BF),
            pltpu.VMEM((Q_ROWS, LMAX), F32),
            pltpu.VMEM((Q_ROWS, LMAX), BF),
            pltpu.VMEM((384, HD), BF),
            pltpu.VMEM((2, 256, 512), F32),
            pltpu.VMEM((2, 2, 128, 512), F32),
            dma((2,)), dma((2,)), dma((2,)), dma((2,)), dma((2,)), dma((2,)), dma, dma,
            dma((2, 9)), dma((2, 9)), dma((1, 9)), dma((1, 9)), dma((2, 9)), dma((2, 9)),
            dma((2, 8)), dma((2, 8)),
        ],
        compiler_params=pltpu.CompilerParams(
            collective_id=0, has_side_effects=True, vmem_limit_bytes=62 * 2**20
        ),
    )(
        query_weight, key_weight, value_weight, output_weight,
        query_amax.reshape(HQ, HD), key_amax.reshape(KVH, HD),
        hidden, positions.reshape(1, -1), cache_keys, cache_values, lengths.reshape(1, -1),
    )
    return result.reshape(hidden.shape[0], 2, 512)


def solution(mesh):
    in_specs = (
        P(("rep", "tp"), None),
        P(("rep", "tp"), None),
        P(("rep", "tp"), None),
        P(("rep", "tp"), None),
        P(),
        P(),
        P("rep", None, None),
        P("rep"),
        P(("rep", "tp"), None, None, None),
        P(("rep", "tp"), None, None, None),
        P(("rep", "tp")),
    )
    out_specs = P("rep", None, "tp")

    def run(*args):
        with jax.sharding.use_abstract_mesh(mesh.abstract_mesh):
            return jax.shard_map(
                body, mesh=mesh, in_specs=in_specs, out_specs=out_specs, check_vma=False
            )(*args)

    return run
```

```python
import jax
import jax.numpy as jnp
from jax import lax
from jax.experimental import pallas as pl
from jax.experimental.pallas import tpu as pltpu
from jax.sharding import PartitionSpec as P

D = 8192
HQ = 32
KVH = 4
HD = 128
LMAX = 256
REP = 8
TP = 16
ROWS = D // (REP * TP)
SEQS = 20
TOKENS = 2 * SEQS
ALL_ROWS = TP * TOKENS
MAIN = 32
TAIL = TOKENS - MAIN
Q_ROWS = SEQS * 16
ROPE_THETA = 1000000.0
MESH = pl.DeviceIdType.MESH
BF = jnp.bfloat16
F32 = jnp.float32


def iota(shape, dim):
    return lax.broadcasted_iota(jnp.int32, shape, dim)


def swap_halves(x):
    return pltpu.roll(x, HD // 2, 1)


def top_half(view):
    return view.at[pl.ds(0, view.shape[0] // 2)]


def bottom_half(view):
    return view.at[pl.ds(view.shape[0] // 2, view.shape[0] // 2)]


def left_half(view):
    return view.at[:, pl.ds(0, view.shape[1] // 2)]


def right_half(view):
    return view.at[:, pl.ds(view.shape[1] // 2, view.shape[1] // 2)]


BY_ROWS = (lambda view: view, top_half, bottom_half)
BY_LANES = (lambda view: view, left_half, right_half)


class Gather:
    ARRIVES = (
        ("x", 0), ("m", 0), ("p", 0), ("xm", 0), ("xp", 0),
        ("2", 1), ("2", 2), ("x2", 1), ("x2", 2),
    )
    SENT = (
        ("own", 0, "x"), ("own", 0, "p"), ("own", 0, "m"), ("x", 0, "p"), ("x", 0, "m"),
        ("m", 1, "p"), ("p", 2, "m"),
    )
    LAST = {
        "pair": (("2", 1, "x"), ("2", 2, "x")),
        "ring": (("xm", 1, "p"), ("xp", 2, "m")),
    }

    def __init__(self, buffers, parts, blocks, neighbours, last, send_sems, recv_sems):
        self.sent = self.SENT + self.LAST[last]
        self.buffers = buffers
        self.parts = parts
        self.blocks = blocks
        self.neighbours = neighbours
        self.send_sems = send_sems
        self.recv_sems = recv_sems
        self.left = set()

    def copies(self, step, arriving):
        if arriving:
            name, part = self.ARRIVES[step]
            device = self.neighbours["x"]
        else:
            name, part, to = self.sent[step]
            device = self.neighbours[to]
        for b, (buffer, parts) in enumerate(zip(self.buffers, self.parts)):
            view = parts[part](buffer(self.blocks[name]))
            yield pltpu.make_async_remote_copy(
                src_ref=view,
                dst_ref=view,
                send_sem=self.send_sems.at[b, step],
                recv_sem=self.recv_sems.at[b, step],
                device_id=device,
                device_id_type=MESH,
            )

    def send(self, *steps):
        for step in steps:
            for copy in self.copies(step, False):
                copy.start()

    def arrive(self, *steps):
        for step in steps:
            for copy in self.copies(step, True):
                copy.wait_recv()

    def leave(self, *steps):
        for step in steps:
            self.left.add(step)
            for copy in self.copies(step, False):
                copy.wait_send()

    def finish(self):
        self.leave(*(step for step in range(9) if step not in self.left))


def kernel(
    wq_ref, wk_ref, wv_ref, wo_ref, qa_ref, ka_ref, hid_ref, pos_ref, ck_ref, cv_ref, len_ref,
    out_ref,
    qf, kvf, wq, kvw, wo_stage, wo, hid, stage, ck, cv, outgoing, incoming, att,
    acc, cosine, sine, pick, unpick, q_g, scores, probs, mixed, main_out, tail_out,
    stage_sems, cache_sems, a_send, a_recv, w_send, w_recv, qkv_send, qkv_recv,
    gq_send, gq_recv, go_send, go_recv, ga_send, ga_recv, core_send, core_recv,
):
    r = lax.axis_index("rep")
    t = lax.axis_index("tp")

    x_rep = lax.rem(r + 4, 8)
    base = r // 4 * 4
    other = 4 - base
    z = lax.rem(r, 4)
    zp, zm, z2 = lax.rem(z + 1, 4), lax.rem(z + 3, 4), lax.rem(z + 2, 4)
    rep_blocks = {
        "own": r, "x": x_rep, "p": base + zp, "m": base + zm, "2": base + z2,
        "xp": other + zp, "xm": other + zm, "x2": other + z2,
    }
    rep_neighbours = {"x": (x_rep, t), "p": (base + zp, t), "m": (base + zm, t)}
    y = t // 4
    low = lax.rem(t, 4)
    far = lax.rem(low + 2, 4)
    yp, ym, y2 = lax.rem(y + 1, 4) * 4, lax.rem(y + 3, 4) * 4, lax.rem(y + 2, 4) * 4
    tp_blocks = {
        "own": t, "x": y * 4 + far, "p": yp + low, "m": ym + low, "2": y2 + low,
        "xp": yp + far, "xm": ym + far, "x2": y2 + far,
    }
    tp_neighbours = {k: (r, tp_blocks[k]) for k in ("x", "p", "m")}
    core = t + 1 - 2 * lax.rem(t, 2)
    barrier = pltpu.get_barrier_semaphore()

    def greet(device):
        pl.semaphore_signal(barrier, inc=1, device_id=device, device_id_type=MESH)

    for k in range(1, TP):
        greet((r, lax.rem(t + k, TP)))
    for k in range(1, REP):
        greet((lax.rem(r + k, REP), t))

    def hidden_copy(i, slot):
        return pltpu.make_async_copy(
            hid_ref.at[:, :, pl.ds(i * 1024, 1024)], stage.at[slot], stage_sems.at[slot]
        )

    hidden_copy(0, 0).start()
    hidden_copy(1, 1).start()

    factors = []
    for g in range(KVH):
        query_peak = jnp.broadcast_to(
            jnp.max(qa_ref[8 * g : 8 * g + 8, :], axis=0, keepdims=True), (8, HD)
        )
        query_peak = jnp.maximum(query_peak, swap_halves(query_peak))
        key_peak = jnp.broadcast_to(ka_ref[g : g + 1, :], (8, HD))
        key_peak = jnp.maximum(key_peak, swap_halves(key_peak))
        factors.append(jnp.sqrt(key_peak / query_peak)[0:1, :])
    for dst in range(TP):
        factor = jnp.concatenate([factors[dst // 4]] * 2, axis=1)
        qf[dst] = (wq_ref[:, 256 * dst : 256 * dst + 256].astype(F32) * factor).astype(BF)
    for g in range(KVH):
        kvf[g] = (wk_ref[:, HD * g : HD * g + HD].astype(F32) / factors[g]).astype(BF)
        kvf[KVH + g] = wv_ref[:, HD * g : HD * g + HD]

    pl.semaphore_wait(barrier, TP - 1 + REP - 1)

    def wo_columns(i):
        return wo_ref.at[:, pl.ds(pl.multiple_of(i * 512, 512), 512)]

    def wo_scatter(k, carry):
        to = lax.rem(r + k, REP)
        pltpu.make_async_remote_copy(
            src_ref=wo_columns(to), dst_ref=wo_stage.at[r],
            send_sem=w_send.at[0], recv_sem=w_recv.at[0],
            device_id=(to, t), device_id_type=MESH,
        ).start()
        return carry


    half = t // 8
    q_rows = pl.ds(pl.multiple_of(t * ROWS, ROWS), ROWS)
    kv_rows = pl.ds(pl.multiple_of(lax.rem(t, 8) * ROWS, ROWS), ROWS)

    def deliver(k, carry):
        dst = lax.rem(t + k, TP)
        pltpu.make_async_remote_copy(
            src_ref=qf.at[dst], dst_ref=wq.at[r, q_rows],
            send_sem=a_send.at[0], recv_sem=a_recv.at[0],
            device_id=(r, dst), device_id_type=MESH,
        ).start()

        @pl.when(lax.rem(dst, 2) == half)
        def _():
            pltpu.make_async_remote_copy(
                src_ref=kvf.at[lax.rem(dst, 4) // 2 * 4 + dst // 4], dst_ref=kvw.at[r, kv_rows],
                send_sem=a_send.at[1], recv_sem=a_recv.at[1],
                device_id=(r, dst), device_id_type=MESH,
            ).start()

        return carry

    lax.fori_loop(1, TP, deliver, 0)
    pltpu.make_async_copy(qf.at[t], wq.at[r, q_rows], a_recv.at[0]).start()
    own_kv = lax.rem(t, 2) == half

    @pl.when(own_kv)
    def _():
        pltpu.make_async_copy(
            kvf.at[lax.rem(t, 4) // 2 * 4 + t // 4], kvw.at[r, kv_rows], a_recv.at[1]
        ).start()

    lax.fori_loop(1, REP, wo_scatter, 0)
    pltpu.make_async_copy(wo_columns(r), wo_stage.at[r], w_recv.at[0]).start()

    wo_rows = pl.ds(pl.multiple_of(lax.rem(t, 8) * ROWS, ROWS), ROWS)

    def wo_deliver(i, carry):
        dst = 2 * i + half

        @pl.when(dst != t)
        def _():
            pltpu.make_async_remote_copy(
                src_ref=wo_stage.at[i], dst_ref=wo.at[r, wo_rows],
                send_sem=w_send.at[1], recv_sem=w_recv.at[1],
                device_id=(r, dst), device_id_type=MESH,
            ).start()

        @pl.when(dst == t)
        def _():
            pltpu.make_async_copy(wo_stage.at[i], wo.at[r, wo_rows], w_recv.at[1]).start()

        return carry

    cache_copies = [
        pltpu.make_async_copy(ck_ref, ck, cache_sems.at[0]),
        pltpu.make_async_copy(cv_ref, cv, cache_sems.at[1]),
    ]

    def relayout(i, carry):
        slot = lax.rem(i, 2)
        hidden_copy(i, slot).wait()
        columns = pl.ds(pl.multiple_of(i * 1024, 1024), 1024)
        hid[:, columns] = stage[slot].reshape(ALL_ROWS, 1024)

        @pl.when(i < 6)
        def _():
            hidden_copy(i + 2, slot).start()

        return carry

    gather_q = Gather(
        [lambda block: wq.at[block], lambda block: kvw.at[block]], [BY_ROWS, BY_ROWS], rep_blocks, rep_neighbours,
        "pair", gq_send, gq_recv,
    )
    gather_o = Gather(
        [lambda block: wo.at[block]], [BY_ROWS], rep_blocks, rep_neighbours, "ring", go_send, go_recv,
    )
    pltpu.make_async_copy(wq.at[r], wq.at[r], a_recv.at[0]).wait()
    pltpu.make_async_copy(kvw.at[r], kvw.at[r], a_recv.at[1]).wait()
    gather_q.send(0, 1, 2)
    pltpu.make_async_copy(wo_stage, wo_stage, w_recv.at[0]).wait()
    lax.fori_loop(0, REP, wo_deliver, 0)
    for copy in cache_copies:
        copy.start()
    lax.fori_loop(0, 8, relayout, 0)

    place = jnp.sum(
        jnp.where(
            iota((ALL_ROWS, 320), 0) // 2 == iota((ALL_ROWS, 320), 1),
            pos_ref[...].reshape(1, TP * SEQS).astype(F32),
            0.0,
        ),
        axis=1,
        keepdims=True,
    ) + lax.rem(iota((ALL_ROWS, 1), 0), 2).astype(F32)
    channel = lax.rem(iota((1, HD), 1), HD // 2).astype(F32)
    angle = place * (ROPE_THETA ** (-2.0 * channel / HD))
    cosine[...] = jnp.cos(angle)
    sine[...] = jnp.sin(angle) * jnp.where(iota((1, HD), 1) < HD // 2, -1.0, 1.0)

    main_out[...] = jnp.zeros_like(main_out)
    tail_out[...] = jnp.zeros_like(tail_out)

    row, col = iota((576, 512), 0), iota((576, 512), 1)
    b, w = row // 16, lax.rem(row, 16)
    source = w // 4 * 128 + lax.rem(w, 2) * TOKENS + 2 * b + lax.rem(w // 2, 2)
    token = lax.rem(row - Q_ROWS + 128, 128)
    col_row, col_dev = lax.rem(col, 128), col // 128
    fresh_row = jnp.logical_and(col_row == 80 + token, token < TOKENS)
    is_key, is_value = row < Q_ROWS + 128, col_dev >= 2
    hit = jnp.where(
        row < Q_ROWS, (col == source).astype(F32),
        jnp.logical_and(fresh_row, is_key != is_value).astype(F32),
    )
    pick[...] = hit.astype(BF)
    row, col = iota((Q_ROWS, 384), 0), iota((Q_ROWS, 384), 1)
    head, token = row // TOKENS, lax.rem(row, TOKENS)
    source = token // 2 * 16 + head // 2 * 4 + lax.rem(token, 2) * 2 + lax.rem(head, 2)
    unpick[...] = (col == source).astype(F32).astype(BF)

    kv_half = lax.rem(t, 2) * 512

    def project(name, first=False):
        block = rep_blocks[name]
        q_at = pl.multiple_of(block * 1024, 1024)
        kv_at = pl.multiple_of(block * 1024 + kv_half, 512)
        for m in range(0, ALL_ROWS, 128):
            q = jnp.dot(hid[m : m + 128, pl.ds(q_at, 1024)], wq[block], preferred_element_type=F32)
            kv = jnp.dot(hid[m : m + 128, pl.ds(kv_at, 512)], kvw[block], preferred_element_type=F32)
            if first:
                acc[m : m + 128, 0:256] = q
                acc[m : m + 128, 256:384] = kv
            else:
                acc[m : m + 128, 0:256] += q
                acc[m : m + 128, 256:384] += kv

    gather_q.arrive(1)
    gather_q.send(5)
    gather_q.arrive(2)
    gather_q.send(6)
    project("own", True)
    gather_q.leave(5, 6)
    gather_q.arrive(0)
    gather_q.send(3, 4)
    pltpu.make_async_copy(wo.at[r], wo.at[r], w_recv.at[1]).wait()
    gather_o.send(0)
    project("m")
    project("p")
    project("x")
    gather_q.arrive(5)
    gather_q.send(7)
    gather_q.arrive(6)
    gather_q.send(8)
    project("2")
    gather_q.arrive(3)
    gather_q.arrive(4)
    gather_o.send(1, 2)
    project("xm")
    project("xp")
    gather_q.arrive(7, 8)
    project("x2")

    is_value_device = lax.rem(t // 2, 2) == 1

    def spread(k, carry):
        dst = lax.rem(t + k, TP)
        rows = pl.ds(pl.multiple_of(dst * TOKENS, 8), TOKENS)
        c, s = cosine[rows, :], sine[rows, :]
        q0, q1, kv = acc[rows, 0:128], acc[rows, 128:256], acc[rows, 256:384]
        q0 = q0 * c + swap_halves(q0) * s
        q1 = q1 * c + swap_halves(q1) * s
        kv = jnp.where(is_value_device, kv, kv * c + swap_halves(kv) * s)
        packed = jnp.concatenate([q0, q1, kv, jnp.zeros((8, HD), F32)], axis=0).astype(BF)
        outgoing[dst] = packed

        @pl.when(k < TP)
        def _():
            pltpu.make_async_remote_copy(
                src_ref=outgoing.at[dst], dst_ref=incoming.at[t],
                send_sem=qkv_send, recv_sem=qkv_recv,
                device_id=(r, dst), device_id_type=MESH,
            ).start()

        @pl.when(k == TP)
        def _():
            pltpu.make_async_copy(outgoing.at[dst], incoming.at[t], qkv_recv).start()

        return carry

    lax.fori_loop(1, TP + 1, spread, 0)
    gather_o.arrive(0)
    gather_o.send(3, 4)

    for copy in cache_copies:
        copy.wait()
    pltpu.make_async_copy(incoming, incoming, qkv_recv).wait()

    lengths = jnp.sum(
        jnp.where(
            iota((Q_ROWS, SEQS), 0) // 16 == iota((Q_ROWS, SEQS), 1), len_ref[...].astype(F32), 0.0
        ),
        axis=1,
        keepdims=True,
    )
    live = iota((Q_ROWS, LMAX), 1).astype(F32) < lengths
    row, col = iota((Q_ROWS, 128), 0), iota((Q_ROWS, 128), 1)
    fresh_live = jnp.logical_and(
        row // 16 == col // 2, lax.rem(col, 2) <= lax.rem(lax.rem(row, 16) // 2, 2)
    )
    mixed[Q_ROWS:384, :] = jnp.zeros((384 - Q_ROWS, HD), BF)

    def attend(g):
        gathered = incoming[pl.ds(g * 4, 4)].reshape(512, HD)
        ordered = jnp.dot(pick[...], gathered, preferred_element_type=F32).astype(BF)
        q_g[...] = ordered[0:Q_ROWS]
        key_new, value_new = ordered[Q_ROWS : Q_ROWS + 128], ordered[Q_ROWS + 128 :]
        for b in range(SEQS):
            scores[16 * b : 16 * b + 16, :] = lax.dot_general(
                q_g[16 * b : 16 * b + 16, :], ck[b, g], (((1,), (1,)), ((), ())),
                preferred_element_type=F32,
            )
        scale = HD ** (-0.5)
        cached = jnp.where(live, scores[...] * scale, -jnp.inf)
        fresh = lax.dot_general(
            q_g[...], key_new, (((1,), (1,)), ((), ())), preferred_element_type=F32
        )
        fresh = jnp.where(fresh_live, fresh * scale, -jnp.inf)
        top = jnp.maximum(
            jnp.max(cached, axis=1, keepdims=True), jnp.max(fresh, axis=1, keepdims=True)
        )
        cached = jnp.exp(cached - top)
        fresh = jnp.exp(fresh - top)
        total = jnp.sum(cached, axis=1, keepdims=True) + jnp.sum(fresh, axis=1, keepdims=True)
        probs[...] = cached.astype(BF)
        fresh_part = jnp.dot(fresh.astype(BF), value_new, preferred_element_type=F32)
        parts = [
            jnp.dot(probs[16 * b : 16 * b + 16, :], cv[b, g], preferred_element_type=F32)
            for b in range(SEQS)
        ]
        mixed[0:Q_ROWS, :] = (
            (jnp.concatenate(parts, axis=0) + fresh_part) / total
        ).astype(BF)
        by_head = jnp.dot(unpick[...], mixed[...], preferred_element_type=F32)
        heads = [by_head[TOKENS * h : TOKENS * h + TOKENS] for h in range(8)]
        last = [x[MAIN:] for x in heads]
        tail = [jnp.concatenate(pair, axis=0) for pair in zip(last[:4], last[4:])]
        att[t, g] = jnp.concatenate(
            [x[:16] for x in heads] + [x[16:MAIN] for x in heads] + tail, axis=1
        ).astype(BF)

    names = ("own", "m", "p", "x", "2", "xm", "xp", "x2")
    gathers = [
        Gather(
            [lambda block, g=g: att.at[block, g]], [BY_LANES], tp_blocks, tp_neighbours, "pair",
            ga_send.at[pl.ds(g, 1)], ga_recv.at[pl.ds(g, 1)],
        )
        for g in range(KVH)
    ]

    def to_core(g, name, block):
        i = names.index(name)
        return pltpu.make_async_remote_copy(
            src_ref=att.at[block, g], dst_ref=att.at[block, g],
            send_sem=core_send.at[g, i], recv_sem=core_recv.at[g, i],
            device_id=(r, core), device_id_type=MESH,
        )

    def share(g, *group):
        for name in group:
            to_core(g, name, tp_blocks[name]).start()

    def first_hop(g):
        gather = gathers[g]
        gather.arrive(1)
        gather.send(5)
        gather.arrive(2)
        gather.send(6)
        gather.arrive(0)
        gather.send(3, 4)
        share(g, "m", "p", "x")

    def second_hop(g):
        gather = gathers[g]
        gather.arrive(5)
        gather.send(7)
        gather.arrive(6)
        gather.send(8)
        share(g, "2")

    def third_hop(g):
        gathers[g].arrive(3)
        share(g, "xm")
        gathers[g].arrive(4)
        share(g, "xp")

    for g in range(KVH):
        attend(g)
        gathers[g].send(0, 1, 2)
        share(g, "own")
        if g == 1:
            gather_o.arrive(1)
            gather_o.send(5)
            gather_o.arrive(2)
            gather_o.send(6)
        if g >= 2:
            first_hop(g - 2)
    second_hop(0)
    first_hop(2)
    second_hop(1)
    first_hop(3)
    gather_o.arrive(3)
    gather_o.send(7)
    gather_o.arrive(4)
    gather_o.send(8)
    second_hop(2)
    second_hop(3)

    chips = {name: tp_blocks[name] // 2 * 2 for name in names}
    flip = 1 - 2 * lax.rem(t, 2)

    def from_core(*group):
        for name in group:
            for g in range(KVH):
                to_core(g, name, tp_blocks[name] + flip).wait_recv()

    def output(i, group, chunks):
        for chunk in chunks:
            block = rep_blocks[chunk]
            g, side = block // 2, lax.rem(block, 2)
            rows = [
                att[pl.ds(chips[name], 2), g, :, lanes].reshape(32, 512)
                for lanes in (
                    pl.ds(pl.multiple_of(side * 512, 512), 512),
                    pl.ds(pl.multiple_of(side * 512 + 1024, 512), 512),
                    pl.ds(2048, 512),
                )
                for name in group
            ]
            product = lax.dot_general(
                jnp.concatenate(rows, axis=0), wo[block], (((1,), (1,)), ((), ())),
                preferred_element_type=F32,
            )
            count = 32 * len(group)
            main_out[i, : 2 * count] += product[: 2 * count]
            tail_out[i, side, :count] += product[2 * count :]

    def store(i, group):
        for n, name in enumerate(group):
            rows = []
            for s in (32 * n, 32 * n + 16):
                rows.append(main_out[i, s : s + 16, :])
                rows.append(main_out[i, 32 * len(group) + s : 32 * len(group) + s + 16, :])
                rows.append(tail_out[i, 0, s : s + 8, :] + tail_out[i, 1, s + 8 : s + 16, :])
            at = pl.ds(chips[name] * SEQS, 2 * SEQS)
            out_ref[at] = jnp.concatenate(rows, axis=0).astype(BF).reshape(2 * SEQS, 2, 512)

    near, distant, last = ("own", "m", "p", "x"), ("2", "xm", "xp"), ("x2",)
    chunks = near + distant + last
    from_core(*near)
    output(0, near, ("own", "m", "p", "x", "xm", "xp"))
    for g in range(KVH):
        third_hop(g)
    gather_o.arrive(5, 6)
    output(0, near, ("2",))
    from_core(*distant)
    output(1, distant, chunks[:-1])
    for g in range(KVH):
        gathers[g].arrive(7, 8)
        share(g, "x2")
    gather_o.arrive(7, 8)
    output(0, near, last)
    store(0, near)
    output(1, distant, last)
    store(1, distant)
    from_core(*last)
    output(2, last, chunks)
    store(2, last)

    def sent_q(k, carry):
        dst = lax.rem(t + k, TP)
        pltpu.make_async_copy(qf.at[dst], qf.at[dst], a_send.at[0]).wait()
        pltpu.make_async_copy(outgoing.at[dst], outgoing.at[dst], qkv_send).wait()

        @pl.when(lax.rem(dst, 2) == half)
        def _():
            pltpu.make_async_copy(kvf.at[0], kvf.at[0], a_send.at[1]).wait()

        return carry

    lax.fori_loop(1, TP, sent_q, 0)

    def sent_o(i, carry):
        pltpu.make_async_copy(wo_stage.at[i], wo_stage.at[i], w_send.at[0]).wait()
        return carry

    lax.fori_loop(1, REP, sent_o, 0)

    def delivered_o(i, carry):
        @pl.when(2 * i + half != t)
        def _():
            pltpu.make_async_copy(wo_stage.at[i], wo_stage.at[i], w_send.at[1]).wait()

        return carry

    lax.fori_loop(0, REP, delivered_o, 0)
    gather_q.finish()
    gather_o.finish()
    for g in range(KVH):
        gathers[g].finish()
        for name in names:
            to_core(g, name, tp_blocks[name]).wait_send()


def body(
    query_weight, key_weight, value_weight, output_weight, query_amax, key_amax,
    hidden, positions, cache_keys, cache_values, lengths,
):
    vmem = pl.BlockSpec(memory_space=pltpu.VMEM)
    hbm = pl.BlockSpec(memory_space=pl.ANY)
    dma = pltpu.SemaphoreType.DMA
    result = pl.pallas_call(
        kernel,
        out_shape=jax.ShapeDtypeStruct((TP * SEQS, 2, 512), BF),
        in_specs=[vmem, vmem, vmem, hbm, vmem, vmem, hbm, vmem, hbm, hbm, vmem],
        out_specs=vmem,
        scratch_shapes=[
            pltpu.VMEM((TP, ROWS, 256), BF),
            pltpu.VMEM((2 * KVH, ROWS, HD), BF),
            pltpu.VMEM((REP, TP * ROWS, 256), BF),
            pltpu.VMEM((REP, 8 * ROWS, HD), BF),
            pltpu.VMEM((REP, ROWS, 512), BF),
            pltpu.VMEM((REP, 512, 512), BF),
            pltpu.VMEM((ALL_ROWS, D), BF),
            pltpu.VMEM((2, 320, 2, 1024), BF),
            pltpu.VMEM((SEQS, KVH, LMAX, HD), BF),
            pltpu.VMEM((SEQS, KVH, LMAX, HD), BF),
            pltpu.VMEM((TP, 128, HD), BF),
            pltpu.VMEM((TP, 128, HD), BF),
            pltpu.VMEM((TP, KVH, 16, 2560), BF),
            pltpu.VMEM((ALL_ROWS, 384), F32),
            pltpu.VMEM((ALL_ROWS, HD), F32),
            pltpu.VMEM((ALL_ROWS, HD), F32),
            pltpu.VMEM((576, 512), BF),
            pltpu.VMEM((Q_ROWS, 384), BF),
            pltpu.VMEM((Q_ROWS, HD), BF),
            pltpu.VMEM((Q_ROWS, LMAX), F32),
            pltpu.VMEM((Q_ROWS, LMAX), BF),
            pltpu.VMEM((384, HD), BF),
            pltpu.VMEM((3, 256, 512), F32),
            pltpu.VMEM((3, 2, 128, 512), F32),
            dma((2,)), dma((2,)), dma((2,)), dma((2,)), dma((2,)), dma((2,)), dma, dma,
            dma((2, 9)), dma((2, 9)), dma((1, 9)), dma((1, 9)), dma((KVH, 9)), dma((KVH, 9)),
            dma((KVH, 8)), dma((KVH, 8)),
        ],
        compiler_params=pltpu.CompilerParams(
            collective_id=0, has_side_effects=True, vmem_limit_bytes=62 * 2**20
        ),
    )(
        query_weight, key_weight, value_weight, output_weight,
        query_amax.reshape(HQ, HD), key_amax.reshape(KVH, HD),
        hidden, positions, cache_keys, cache_values, lengths.reshape(1, -1),
    )
    return result


def solution(mesh):
    in_specs = (
        P(("rep", "tp"), None),
        P(("rep", "tp"), None),
        P(("rep", "tp"), None),
        P(("rep", "tp"), None),
        P(),
        P(),
        P("rep", None, None),
        P("rep"),
        P(("rep", "tp"), None, None, None),
        P(("rep", "tp"), None, None, None),
        P(("rep", "tp")),
    )
    out_specs = P("rep", None, "tp")

    def run(*args):
        with jax.sharding.use_abstract_mesh(mesh.abstract_mesh):
            return jax.shard_map(
                body, mesh=mesh, in_specs=in_specs, out_specs=out_specs, check_vma=False
            )(*args)

    return run
```

```python
import jax
import jax.numpy as jnp
from jax import lax
from jax.experimental import pallas as pl
from jax.experimental.pallas import tpu as pltpu
from jax.sharding import PartitionSpec as P

D = 8192
HQ = 32
KVH = 4
HD = 128
LMAX = 256
REP = 8
TP = 16
ROWS = D // (REP * TP)
SEQS = 20
TOKENS = 2 * SEQS
ALL_ROWS = TP * TOKENS
MAIN = 32
TAIL = TOKENS - MAIN
Q_ROWS = SEQS * 16
ROPE_THETA = 1000000.0
MESH = pl.DeviceIdType.MESH
BF = jnp.bfloat16
F32 = jnp.float32


def iota(shape, dim):
    return lax.broadcasted_iota(jnp.int32, shape, dim)


def swap_halves(x):
    return pltpu.roll(x, HD // 2, 1)


def top_half(view):
    return view.at[pl.ds(0, view.shape[0] // 2)]


def bottom_half(view):
    return view.at[pl.ds(view.shape[0] // 2, view.shape[0] // 2)]


def left_half(view):
    return view.at[:, pl.ds(0, view.shape[1] // 2)]


def right_half(view):
    return view.at[:, pl.ds(view.shape[1] // 2, view.shape[1] // 2)]


def top_part(view):
    return view.at[pl.ds(0, view.shape[0] * 3 // 16)]


def bottom_part(view):
    return view.at[pl.ds(view.shape[0] * 3 // 16, view.shape[0] * 13 // 16)]


BY_ROWS = (lambda view: view, top_half, bottom_half, top_part, bottom_part)
BY_LANES = (lambda view: view, left_half, right_half)


FIRST = (("own", 0, "x", "x"), ("own", 0, "p", "m"), ("own", 0, "m", "p"))
WHOLE = (("x", 0, "p", "xm"), ("x", 0, "m", "xp"))
LESS = (("x", 4, "p", "xm"), ("x", 4, "m", "xp"))
HALVES = (("m", 1, "p", "2"), ("p", 2, "m", "2"))
PAIR = FIRST + WHOLE + HALVES + (("2", 1, "x", "x2"), ("2", 2, "x", "x2"))
RING = FIRST + WHOLE + HALVES + (("xm", 1, "p", "x2"), ("xp", 2, "m", "x2"))
BOTH = FIRST + WHOLE + HALVES + (("2", 1, "x", "x2"), ("xp", 2, "m", "x2"))
MIXED = (
    FIRST + LESS + HALVES
    + (("2", 1, "x", "x2"), ("2", 2, "x", "x2"), ("m", 3, "x", "xm"), ("p", 3, "x", "xp"))
)


class Gather:
    def __init__(self, plan, buffers, parts, blocks, neighbours, send_sems, recv_sems):
        self.plan = plan
        self.buffers = buffers
        self.parts = parts
        self.blocks = blocks
        self.neighbours = neighbours
        self.send_sems = send_sems
        self.recv_sems = recv_sems
        self.left = set()

    def copies(self, step, arriving):
        name, part, to, there = self.plan[step]
        name = there if arriving else name
        device = self.neighbours[to]
        for b, (buffer, parts) in enumerate(zip(self.buffers, self.parts)):
            view = parts[part](buffer(self.blocks[name]))
            yield pltpu.make_async_remote_copy(
                src_ref=view,
                dst_ref=view,
                send_sem=self.send_sems.at[b, step],
                recv_sem=self.recv_sems.at[b, step],
                device_id=device,
                device_id_type=MESH,
            )

    def send(self, *steps):
        for step in steps:
            for copy in self.copies(step, False):
                copy.start()

    def arrive(self, *steps):
        for step in steps:
            for copy in self.copies(step, True):
                copy.wait_recv()

    def leave(self, *steps):
        for step in steps:
            self.left.add(step)
            for copy in self.copies(step, False):
                copy.wait_send()

    def finish(self):
        self.leave(*(step for step in range(len(self.plan)) if step not in self.left))


def kernel(
    wq_ref, wk_ref, wv_ref, wo_ref, qa_ref, ka_ref, hid_ref, pos_ref, ck_ref, cv_ref, len_ref,
    out_ref,
    qf, qf2, kvf, wq, wq2, kvw, wo_stage, wo, hid, stage, ck, cv, outgoing, outgoing2, incoming, incoming2, att,
    acc, cosine, sine, pick, unpick, q_g, scores, probs, mixed, main_out, tail_out,
    stage_sems, cache_sems, a_send, a_recv, w_send, w_recv, qkv_send, qkv_recv,
    gq_send, gq_recv, gr_send, gr_recv, go_send, go_recv, ga_send, ga_recv, core_send, core_recv,
):
    r = lax.axis_index("rep")
    t = lax.axis_index("tp")

    x_rep = lax.rem(r + 4, 8)
    base = r // 4 * 4
    other = 4 - base
    z = lax.rem(r, 4)
    zp, zm, z2 = lax.rem(z + 1, 4), lax.rem(z + 3, 4), lax.rem(z + 2, 4)
    rep_blocks = {
        "own": r, "x": x_rep, "p": base + zp, "m": base + zm, "2": base + z2,
        "xp": other + zp, "xm": other + zm, "x2": other + z2,
    }
    rep_neighbours = {"x": (x_rep, t), "p": (base + zp, t), "m": (base + zm, t)}
    side = lax.rem(t // 2, 2)

    def across(other_side, rep):
        return jnp.where(other_side != side, lax.rem(rep + 4, 8), rep)

    y = t // 4
    low = lax.rem(t, 4)
    far = lax.rem(low + 2, 4)
    yp, ym, y2 = lax.rem(y + 1, 4) * 4, lax.rem(y + 3, 4) * 4, lax.rem(y + 2, 4) * 4
    tp_blocks = {
        "own": t, "x": y * 4 + far, "p": yp + low, "m": ym + low, "2": y2 + low,
        "xp": yp + far, "xm": ym + far, "x2": y2 + far,
    }
    tp_neighbours = {k: (r, tp_blocks[k]) for k in ("x", "p", "m")}
    core = t + 1 - 2 * lax.rem(t, 2)
    barrier = pltpu.get_barrier_semaphore()

    def greet(device):
        pl.semaphore_signal(barrier, inc=1, device_id=device, device_id_type=MESH)

    for k in range(1, TP):
        greet((r, lax.rem(t + k, TP)))
    for k in range(1, REP):
        greet((lax.rem(r + k, REP), t))
    for k in range(8):
        greet((x_rep, k // 2 * 4 + 2 - side * 2 + k % 2))

    def hidden_copy(i, slot):
        return pltpu.make_async_copy(
            hid_ref.at[:, :, pl.ds(i * 1024, 1024)], stage.at[slot], stage_sems.at[slot]
        )

    hidden_copy(0, 0).start()
    hidden_copy(1, 1).start()

    factors = []
    for g in range(KVH):
        query_peak = jnp.broadcast_to(
            jnp.max(qa_ref[8 * g : 8 * g + 8, :], axis=0, keepdims=True), (8, HD)
        )
        query_peak = jnp.maximum(query_peak, swap_halves(query_peak))
        key_peak = jnp.broadcast_to(ka_ref[g : g + 1, :], (8, HD))
        key_peak = jnp.maximum(key_peak, swap_halves(key_peak))
        factors.append(jnp.sqrt(key_peak / query_peak)[0:1, :])
    for dst in range(TP):
        for n, folded in enumerate((qf, qf2)):
            at = 256 * dst + HD * n
            folded[dst] = (wq_ref[:, at : at + HD].astype(F32) * factors[dst // 4]).astype(BF)
    for g in range(KVH):
        kvf[g] = (wk_ref[:, HD * g : HD * g + HD].astype(F32) / factors[g]).astype(BF)
        kvf[KVH + g] = wv_ref[:, HD * g : HD * g + HD]

    pl.semaphore_wait(barrier, TP - 1 + REP - 1 + 8)

    def wo_columns(i):
        return wo_ref.at[:, pl.ds(pl.multiple_of(i * 512, 512), 512)]

    def wo_scatter(k, carry):
        to = lax.rem(r + k, REP)
        pltpu.make_async_remote_copy(
            src_ref=wo_columns(across(lax.rem(r, 2), to)), dst_ref=wo_stage.at[r],
            send_sem=w_send.at[0], recv_sem=w_recv.at[0],
            device_id=(to, t), device_id_type=MESH,
        ).start()
        return carry


    half = t // 8
    q_rows = pl.ds(pl.multiple_of(t * ROWS, ROWS), ROWS)
    kv_rows = pl.ds(pl.multiple_of(lax.rem(t, 8) * ROWS, ROWS), ROWS)

    def deliver(k, carry):
        dst = lax.rem(t + k, TP)
        rep = across(lax.rem(dst // 2, 2), r)
        pltpu.make_async_remote_copy(
            src_ref=qf.at[dst], dst_ref=wq.at[rep, q_rows],
            send_sem=a_send.at[0], recv_sem=a_recv.at[0],
            device_id=(rep, dst), device_id_type=MESH,
        ).start()

        @pl.when(lax.rem(dst, 2) == half)
        def _():
            pltpu.make_async_remote_copy(
                src_ref=kvf.at[lax.rem(dst, 4) // 2 * 4 + dst // 4], dst_ref=kvw.at[rep, kv_rows],
                send_sem=a_send.at[1], recv_sem=a_recv.at[1],
                device_id=(rep, dst), device_id_type=MESH,
            ).start()

        return carry

    def deliver_second(k, carry):
        dst = lax.rem(t + k, TP)
        rep = across(lax.rem(dst // 2, 2), r)
        pltpu.make_async_remote_copy(
            src_ref=qf2.at[dst], dst_ref=wq2.at[rep, q_rows],
            send_sem=a_send.at[2], recv_sem=a_recv.at[2],
            device_id=(rep, dst), device_id_type=MESH,
        ).start()
        return carry

    lax.fori_loop(1, TP, deliver, 0)
    pltpu.make_async_copy(qf.at[t], wq.at[r, q_rows], a_recv.at[0]).start()
    own_kv = lax.rem(t, 2) == half

    @pl.when(own_kv)
    def _():
        pltpu.make_async_copy(
            kvf.at[lax.rem(t, 4) // 2 * 4 + t // 4], kvw.at[r, kv_rows], a_recv.at[1]
        ).start()

    lax.fori_loop(1, TP, deliver_second, 0)
    pltpu.make_async_copy(qf2.at[t], wq2.at[r, q_rows], a_recv.at[2]).start()
    lax.fori_loop(1, REP, wo_scatter, 0)
    pltpu.make_async_copy(wo_columns(across(lax.rem(r, 2), r)), wo_stage.at[r], w_recv.at[0]).start()

    wo_rows = pl.ds(pl.multiple_of(lax.rem(t, 8) * ROWS, ROWS), ROWS)

    def wo_deliver(i, carry):
        dst = 2 * i + half
        rep = across(lax.rem(i, 2), r)

        @pl.when(dst != t)
        def _():
            pltpu.make_async_remote_copy(
                src_ref=wo_stage.at[i], dst_ref=wo.at[rep, wo_rows],
                send_sem=w_send.at[1], recv_sem=w_recv.at[1],
                device_id=(rep, dst), device_id_type=MESH,
            ).start()

        @pl.when(dst == t)
        def _():
            pltpu.make_async_copy(wo_stage.at[i], wo.at[r, wo_rows], w_recv.at[1]).start()

        return carry

    cache_copies = [
        pltpu.make_async_copy(ck_ref, ck, cache_sems.at[0]),
        pltpu.make_async_copy(cv_ref, cv, cache_sems.at[1]),
    ]

    def relayout(i, carry):
        slot = lax.rem(i, 2)
        hidden_copy(i, slot).wait()
        block = stage[slot].reshape(ALL_ROWS, 1024)
        for n in range(8):
            at = pl.multiple_of(across(n % 2, i) * 1024 + n * 128, 128)
            hid[:, pl.ds(at, 128)] = block[:, n * 128 : n * 128 + 128]

        @pl.when(i < 6)
        def _():
            hidden_copy(i + 2, slot).start()

        return carry

    gather_q = Gather(
        PAIR,
        [lambda block: wq.at[block], lambda block: kvw.at[block]], [BY_ROWS, BY_ROWS], rep_blocks, rep_neighbours,
        gq_send, gq_recv,
    )
    gather_r = Gather(
        PAIR, [lambda block: wq2.at[block]], [BY_ROWS], rep_blocks, rep_neighbours,
        gr_send, gr_recv,
    )
    gather_o = Gather(
        RING,
        [lambda block: wo.at[block]], [BY_ROWS], rep_blocks, rep_neighbours, go_send, go_recv,
    )
    pltpu.make_async_copy(wq.at[r], wq.at[r], a_recv.at[0]).wait()
    pltpu.make_async_copy(kvw.at[r], kvw.at[r], a_recv.at[1]).wait()
    gather_q.send(0, 1, 2)
    pltpu.make_async_copy(wq2.at[r], wq2.at[r], a_recv.at[2]).wait()
    gather_r.send(0, 1, 2)
    pltpu.make_async_copy(wo_stage, wo_stage, w_recv.at[0]).wait()
    lax.fori_loop(0, REP, wo_deliver, 0)
    for copy in cache_copies:
        copy.start()
    lax.fori_loop(0, 8, relayout, 0)

    place = jnp.sum(
        jnp.where(
            iota((ALL_ROWS, 320), 0) // 2 == iota((ALL_ROWS, 320), 1),
            pos_ref[...].reshape(1, TP * SEQS).astype(F32),
            0.0,
        ),
        axis=1,
        keepdims=True,
    ) + lax.rem(iota((ALL_ROWS, 1), 0), 2).astype(F32)
    channel = lax.rem(iota((1, HD), 1), HD // 2).astype(F32)
    angle = place * (ROPE_THETA ** (-2.0 * channel / HD))
    cosine[...] = jnp.cos(angle)
    sine[...] = jnp.sin(angle) * jnp.where(iota((1, HD), 1) < HD // 2, -1.0, 1.0)

    main_out[...] = jnp.zeros_like(main_out)
    tail_out[...] = jnp.zeros_like(tail_out)

    row, col = iota((576, 512), 0), iota((576, 512), 1)
    b, w = row // 16, lax.rem(row, 16)
    token = 2 * b + lax.rem(w // 2, 2)
    source = w // 4 * 80 + token
    source = jnp.where(lax.rem(w, 2) == 0, source, 320 + w // 4 * 48 + token)
    token = lax.rem(row - Q_ROWS + 128, 128)
    fresh_row = jnp.logical_and(
        jnp.logical_and(col < 320, lax.rem(col, 80) == TOKENS + token), token < TOKENS
    )
    is_key, is_value = row < Q_ROWS + 128, col >= 160
    hit = jnp.where(
        row < Q_ROWS, (col == source).astype(F32),
        jnp.logical_and(fresh_row, is_key != is_value).astype(F32),
    )
    pick[...] = hit.astype(BF)
    row, col = iota((Q_ROWS, 384), 0), iota((Q_ROWS, 384), 1)
    head, token = row // TOKENS, lax.rem(row, TOKENS)
    source = token // 2 * 16 + head // 2 * 4 + lax.rem(token, 2) * 2 + lax.rem(head, 2)
    unpick[...] = (col == source).astype(F32).astype(BF)

    kv_half = lax.rem(t, 2) * 512

    def project(name, first=False):
        block = rep_blocks[name]
        q_at = pl.multiple_of(block * 1024, 1024)
        kv_at = pl.multiple_of(block * 1024 + kv_half, 512)
        for m in range(0, ALL_ROWS, 128):
            q = jnp.dot(hid[m : m + 128, pl.ds(q_at, 1024)], wq[block], preferred_element_type=F32)
            kv = jnp.dot(hid[m : m + 128, pl.ds(kv_at, 512)], kvw[block], preferred_element_type=F32)
            if first:
                acc[m : m + 128, 0:128] = q
                acc[m : m + 128, 256:384] = kv
            else:
                acc[m : m + 128, 0:128] += q
                acc[m : m + 128, 256:384] += kv

    def project_second(name, first=False):
        block = rep_blocks[name]
        q_at = pl.multiple_of(block * 1024, 1024)
        for m in range(0, ALL_ROWS, 128):
            q = jnp.dot(hid[m : m + 128, pl.ds(q_at, 1024)], wq2[block], preferred_element_type=F32)
            if first:
                acc[m : m + 128, 128:256] = q
            else:
                acc[m : m + 128, 128:256] += q

    is_value_device = lax.rem(t // 2, 2) == 1

    def rotate(x, rows):
        return x * cosine[rows, :] + swap_halves(x) * sine[rows, :]

    def to_owner(buffer, landing, i, k):
        dst = lax.rem(t + k, TP)

        @pl.when(k < TP)
        def _():
            pltpu.make_async_remote_copy(
                src_ref=buffer.at[dst], dst_ref=landing.at[t],
                send_sem=qkv_send.at[i], recv_sem=qkv_recv.at[i],
                device_id=(r, dst), device_id_type=MESH,
            ).start()

        @pl.when(k == TP)
        def _():
            pltpu.make_async_copy(buffer.at[dst], landing.at[t], qkv_recv.at[i]).start()

    def spread(k, carry):
        dst = lax.rem(t + k, TP)
        rows = pl.ds(pl.multiple_of(dst * TOKENS, 8), TOKENS)
        kv = acc[rows, 256:384]
        kv = jnp.where(is_value_device, kv, rotate(kv, rows))
        outgoing[dst] = jnp.concatenate([rotate(acc[rows, 0:128], rows), kv], axis=0).astype(BF)
        to_owner(outgoing, incoming, 0, k)
        return carry

    def spread_second(k, carry):
        dst = lax.rem(t + k, TP)
        rows = pl.ds(pl.multiple_of(dst * TOKENS, 8), TOKENS)
        q = rotate(acc[rows, 128:256], rows)
        outgoing2[dst] = jnp.concatenate([q, jnp.zeros((8, HD), F32)], axis=0).astype(BF)
        to_owner(outgoing2, incoming2, 1, k)
        return carry

    gather_q.arrive(1)
    gather_q.send(5)
    gather_q.arrive(2)
    gather_q.send(6)
    project("own", True)
    project_second("own", True)
    gather_q.leave(5, 6)
    gather_q.arrive(0)
    gather_q.send(3, 4)
    gather_r.arrive(1)
    gather_r.send(5)
    gather_r.arrive(2)
    gather_r.send(6)
    gather_r.arrive(0)
    gather_r.send(3, 4)
    project("m")
    project("p")
    project("x")
    gather_q.arrive(5)
    gather_q.send(7)
    gather_q.arrive(6)
    gather_q.send(8)
    project("2")
    pltpu.make_async_copy(wo.at[r], wo.at[r], w_recv.at[1]).wait()
    gather_o.send(0)
    project_second("m")
    project_second("p")
    project_second("x")
    gather_r.arrive(5)
    gather_r.send(7)
    gather_r.arrive(6)
    gather_r.send(8)
    gather_q.arrive(3)
    project("xm")
    gather_q.arrive(4)
    project("xp")
    gather_q.arrive(7, 8)
    project("x2")
    lax.fori_loop(1, TP + 1, spread, 0)
    project_second("2")
    gather_r.arrive(3)
    gather_r.arrive(4)
    gather_o.send(1, 2)
    project_second("xm")
    project_second("xp")
    gather_r.arrive(7, 8)
    project_second("x2")
    lax.fori_loop(1, TP + 1, spread_second, 0)
    gather_o.arrive(0)
    gather_o.send(3, 4)

    for copy in cache_copies:
        copy.wait()
    pltpu.make_async_copy(incoming, incoming, qkv_recv.at[0]).wait()
    pltpu.make_async_copy(incoming2, incoming2, qkv_recv.at[1]).wait()

    lengths = jnp.sum(
        jnp.where(
            iota((Q_ROWS, SEQS), 0) // 16 == iota((Q_ROWS, SEQS), 1), len_ref[...].astype(F32), 0.0
        ),
        axis=1,
        keepdims=True,
    )
    live = iota((Q_ROWS, LMAX), 1).astype(F32) < lengths
    row, col = iota((Q_ROWS, 128), 0), iota((Q_ROWS, 128), 1)
    fresh_live = jnp.logical_and(
        row // 16 == col // 2, lax.rem(col, 2) <= lax.rem(lax.rem(row, 16) // 2, 2)
    )
    mixed[Q_ROWS:384, :] = jnp.zeros((384 - Q_ROWS, HD), BF)

    def attend(g):
        gathered = jnp.concatenate(
            [
                incoming[pl.ds(g * 4, 4)].reshape(8 * TOKENS, HD),
                incoming2[pl.ds(g * 4, 4)].reshape(192, HD),
            ],
            axis=0,
        )
        ordered = jnp.dot(pick[...], gathered, preferred_element_type=F32).astype(BF)
        q_g[...] = ordered[0:Q_ROWS]
        key_new, value_new = ordered[Q_ROWS : Q_ROWS + 128], ordered[Q_ROWS + 128 :]
        for b in range(SEQS):
            scores[16 * b : 16 * b + 16, :] = lax.dot_general(
                q_g[16 * b : 16 * b + 16, :], ck[b, g], (((1,), (1,)), ((), ())),
                preferred_element_type=F32,
            )
        scale = HD ** (-0.5)
        cached = jnp.where(live, scores[...] * scale, -jnp.inf)
        fresh = lax.dot_general(
            q_g[...], key_new, (((1,), (1,)), ((), ())), preferred_element_type=F32
        )
        fresh = jnp.where(fresh_live, fresh * scale, -jnp.inf)
        top = jnp.maximum(
            jnp.max(cached, axis=1, keepdims=True), jnp.max(fresh, axis=1, keepdims=True)
        )
        cached = jnp.exp(cached - top)
        fresh = jnp.exp(fresh - top)
        total = jnp.sum(cached, axis=1, keepdims=True) + jnp.sum(fresh, axis=1, keepdims=True)
        probs[...] = cached.astype(BF)
        fresh_part = jnp.dot(fresh.astype(BF), value_new, preferred_element_type=F32)
        parts = [
            jnp.dot(probs[16 * b : 16 * b + 16, :], cv[b, g], preferred_element_type=F32)
            for b in range(SEQS)
        ]
        mixed[0:Q_ROWS, :] = (
            (jnp.concatenate(parts, axis=0) + fresh_part) / total
        ).astype(BF)
        by_head = jnp.dot(unpick[...], mixed[...], preferred_element_type=F32)
        heads = [by_head[TOKENS * h : TOKENS * h + TOKENS] for h in range(8)]
        last = [x[MAIN:] for x in heads]
        tail = [jnp.concatenate(pair, axis=0) for pair in zip(last[:4], last[4:])]
        att[t, g] = jnp.concatenate(
            [x[:16] for x in heads] + [x[16:MAIN] for x in heads] + tail, axis=1
        ).astype(BF)

    names = ("own", "m", "p", "x", "2", "xm", "xp", "x2")
    gathers = [
        Gather(
            PAIR,
            [lambda block, g=g: att.at[block, g]], [BY_LANES], tp_blocks, tp_neighbours,
            ga_send.at[pl.ds(g, 1)], ga_recv.at[pl.ds(g, 1)],
        )
        for g in range(KVH)
    ]

    def to_core(g, name, block):
        i = names.index(name)
        return pltpu.make_async_remote_copy(
            src_ref=att.at[block, g], dst_ref=att.at[block, g],
            send_sem=core_send.at[g, i], recv_sem=core_recv.at[g, i],
            device_id=(r, core), device_id_type=MESH,
        )

    def share(g, *group):
        for name in group:
            to_core(g, name, tp_blocks[name]).start()

    def first_hop(g):
        gather = gathers[g]
        gather.arrive(1)
        gather.send(5)
        gather.arrive(2)
        gather.send(6)
        gather.arrive(0)
        gather.send(3, 4)
        share(g, "m", "p", "x")

    def second_hop(g):
        gather = gathers[g]
        gather.arrive(5)
        gather.send(7)
        gather.arrive(6)
        gather.send(8)
        share(g, "2")

    def third_hop(g):
        gathers[g].arrive(3)
        share(g, "xm")
        gathers[g].arrive(4)
        share(g, "xp")

    for g in range(KVH):
        attend(g)
        gathers[g].send(0, 1, 2)
        share(g, "own")
        if g == 0:
            gather_o.arrive(1)
            gather_o.send(5)
            gather_o.arrive(2)
            gather_o.send(6)
        if g >= 2:
            first_hop(g - 2)
    gather_o.arrive(3)
    gather_o.send(7)
    gather_o.arrive(4)
    gather_o.send(8)
    second_hop(0)
    first_hop(2)
    second_hop(1)
    first_hop(3)
    second_hop(2)
    second_hop(3)

    chips = {name: tp_blocks[name] // 2 * 2 for name in names}
    flip = 1 - 2 * lax.rem(t, 2)

    def from_core(*group):
        for name in group:
            for g in range(KVH):
                to_core(g, name, tp_blocks[name] + flip).wait_recv()

    def output(i, group, chunks):
        for chunk in chunks:
            block = rep_blocks[chunk]
            g, side = block // 2, lax.rem(block, 2)
            rows = [
                att[pl.ds(chips[name], 2), g, :, lanes].reshape(32, 512)
                for lanes in (
                    pl.ds(pl.multiple_of(side * 512, 512), 512),
                    pl.ds(pl.multiple_of(side * 512 + 1024, 512), 512),
                    pl.ds(2048, 512),
                )
                for name in group
            ]
            product = lax.dot_general(
                jnp.concatenate(rows, axis=0), wo[block], (((1,), (1,)), ((), ())),
                preferred_element_type=F32,
            )
            count = 32 * len(group)
            main_out[i, : 2 * count] += product[: 2 * count]
            tail_out[i, side, :count] += product[2 * count :]

    def store(i, group):
        for n, name in enumerate(group):
            rows = []
            for s in (32 * n, 32 * n + 16):
                rows.append(main_out[i, s : s + 16, :])
                rows.append(main_out[i, 32 * len(group) + s : 32 * len(group) + s + 16, :])
                rows.append(tail_out[i, 0, s : s + 8, :] + tail_out[i, 1, s + 8 : s + 16, :])
            at = pl.ds(chips[name] * SEQS, 2 * SEQS)
            out_ref[at] = jnp.concatenate(rows, axis=0).astype(BF).reshape(2 * SEQS, 2, 512)

    near, distant, last = ("own", "m", "p", "x"), ("2", "xm", "xp"), ("x2",)
    chunks = near + distant + last
    from_core(*near)
    output(0, near, ("own", "m", "p", "x", "xm", "xp"))
    for g in range(KVH):
        third_hop(g)
    gather_o.arrive(5, 6)
    output(0, near, ("2",))
    from_core(*distant)
    output(1, distant, chunks[:-1])
    for g in range(KVH):
        gathers[g].arrive(7, 8)
        share(g, "x2")
    gather_o.arrive(7, 8)
    output(0, near, last)
    store(0, near)
    output(1, distant, last)
    store(1, distant)
    from_core(*last)
    output(2, last, chunks)
    store(2, last)

    def sent_q(k, carry):
        dst = lax.rem(t + k, TP)
        pltpu.make_async_copy(qf.at[dst], qf.at[dst], a_send.at[0]).wait()
        pltpu.make_async_copy(qf2.at[dst], qf2.at[dst], a_send.at[2]).wait()
        pltpu.make_async_copy(outgoing.at[dst], outgoing.at[dst], qkv_send.at[0]).wait()
        pltpu.make_async_copy(outgoing2.at[dst], outgoing2.at[dst], qkv_send.at[1]).wait()

        @pl.when(lax.rem(dst, 2) == half)
        def _():
            pltpu.make_async_copy(kvf.at[0], kvf.at[0], a_send.at[1]).wait()

        return carry

    lax.fori_loop(1, TP, sent_q, 0)

    def sent_o(i, carry):
        pltpu.make_async_copy(wo_stage.at[i], wo_stage.at[i], w_send.at[0]).wait()
        return carry

    lax.fori_loop(1, REP, sent_o, 0)

    def delivered_o(i, carry):
        @pl.when(2 * i + half != t)
        def _():
            pltpu.make_async_copy(wo_stage.at[i], wo_stage.at[i], w_send.at[1]).wait()

        return carry

    lax.fori_loop(0, REP, delivered_o, 0)
    gather_q.finish()
    gather_r.finish()
    gather_o.finish()
    for g in range(KVH):
        gathers[g].finish()
        for name in names:
            to_core(g, name, tp_blocks[name]).wait_send()


def body(
    query_weight, key_weight, value_weight, output_weight, query_amax, key_amax,
    hidden, positions, cache_keys, cache_values, lengths,
):
    vmem = pl.BlockSpec(memory_space=pltpu.VMEM)
    hbm = pl.BlockSpec(memory_space=pl.ANY)
    dma = pltpu.SemaphoreType.DMA
    result = pl.pallas_call(
        kernel,
        out_shape=jax.ShapeDtypeStruct((TP * SEQS, 2, 512), BF),
        in_specs=[vmem, vmem, vmem, hbm, vmem, vmem, hbm, vmem, hbm, hbm, vmem],
        out_specs=vmem,
        scratch_shapes=[
            pltpu.VMEM((TP, ROWS, HD), BF),
            pltpu.VMEM((TP, ROWS, HD), BF),
            pltpu.VMEM((2 * KVH, ROWS, HD), BF),
            pltpu.VMEM((REP, TP * ROWS, HD), BF),
            pltpu.VMEM((REP, TP * ROWS, HD), BF),
            pltpu.VMEM((REP, 8 * ROWS, HD), BF),
            pltpu.VMEM((REP, ROWS, 512), BF),
            pltpu.VMEM((REP, 512, 512), BF),
            pltpu.VMEM((ALL_ROWS, D), BF),
            pltpu.VMEM((2, 320, 2, 1024), BF),
            pltpu.VMEM((SEQS, KVH, LMAX, HD), BF),
            pltpu.VMEM((SEQS, KVH, LMAX, HD), BF),
            pltpu.VMEM((TP, 80, HD), BF),
            pltpu.VMEM((TP, 48, HD), BF),
            pltpu.VMEM((TP, 80, HD), BF),
            pltpu.VMEM((TP, 48, HD), BF),
            pltpu.VMEM((TP, KVH, 16, 2560), BF),
            pltpu.VMEM((ALL_ROWS, 384), F32),
            pltpu.VMEM((ALL_ROWS, HD), F32),
            pltpu.VMEM((ALL_ROWS, HD), F32),
            pltpu.VMEM((576, 512), BF),
            pltpu.VMEM((Q_ROWS, 384), BF),
            pltpu.VMEM((Q_ROWS, HD), BF),
            pltpu.VMEM((Q_ROWS, LMAX), F32),
            pltpu.VMEM((Q_ROWS, LMAX), BF),
            pltpu.VMEM((384, HD), BF),
            pltpu.VMEM((3, 256, 512), F32),
            pltpu.VMEM((3, 2, 128, 512), F32),
            dma((2,)), dma((2,)), dma((3,)), dma((3,)), dma((2,)), dma((2,)), dma((2,)), dma((2,)),
            dma((2, 11)), dma((2, 11)), dma((1, 9)), dma((1, 9)), dma((1, 9)), dma((1, 9)), dma((KVH, 9)), dma((KVH, 9)),
            dma((KVH, 8)), dma((KVH, 8)),
        ],
        compiler_params=pltpu.CompilerParams(
            collective_id=0, has_side_effects=True, vmem_limit_bytes=62 * 2**20
        ),
    )(
        query_weight, key_weight, value_weight, output_weight,
        query_amax.reshape(HQ, HD), key_amax.reshape(KVH, HD),
        hidden, positions, cache_keys, cache_values, lengths.reshape(1, -1),
    )
    return result


def solution(mesh):
    in_specs = (
        P(("rep", "tp"), None),
        P(("rep", "tp"), None),
        P(("rep", "tp"), None),
        P(("rep", "tp"), None),
        P(),
        P(),
        P("rep", None, None),
        P("rep"),
        P(("rep", "tp"), None, None, None),
        P(("rep", "tp"), None, None, None),
        P(("rep", "tp")),
    )
    out_specs = P("rep", None, "tp")

    def run(*args):
        with jax.sharding.use_abstract_mesh(mesh.abstract_mesh):
            return jax.shard_map(
                body, mesh=mesh, in_specs=in_specs, out_specs=out_specs, check_vma=False
            )(*args)

    return run
```

```python
import jax
import jax.numpy as jnp
from jax import lax
from jax.experimental import pallas as pl
from jax.experimental.pallas import tpu as pltpu
from jax.sharding import PartitionSpec as P

D = 8192
HQ = 32
KVH = 4
HD = 128
LMAX = 256
REP = 8
TP = 16
ROWS = D // (REP * TP)
SEQS = 20
TOKENS = 2 * SEQS
ALL_ROWS = TP * TOKENS
MAIN = 32
TAIL = TOKENS - MAIN
H_ROWS = SEQS * 8
ROPE_THETA = 1000000.0
MESH = pl.DeviceIdType.MESH
BF = jnp.bfloat16
F32 = jnp.float32


def iota(shape, dim):
    return lax.broadcasted_iota(jnp.int32, shape, dim)


def swap_halves(x):
    return pltpu.roll(x, HD // 2, 1)


def top_half(view):
    return view.at[pl.ds(0, view.shape[0] // 2)]


def bottom_half(view):
    return view.at[pl.ds(view.shape[0] // 2, view.shape[0] // 2)]


def left_half(view):
    return view.at[:, pl.ds(0, view.shape[1] // 2)]


def right_half(view):
    return view.at[:, pl.ds(view.shape[1] // 2, view.shape[1] // 2)]


BY_ROWS = (lambda view: view, top_half, bottom_half)
BY_LANES = (lambda view: view, left_half, right_half)


FIRST = (("own", 0, "x", "x"), ("own", 0, "p", "m"), ("own", 0, "m", "p"))
WHOLE = (("x", 0, "p", "xm"), ("x", 0, "m", "xp"))
HALVES = (("m", 1, "p", "2"), ("p", 2, "m", "2"))
PAIR = FIRST + WHOLE + HALVES + (("2", 1, "x", "x2"), ("2", 2, "x", "x2"))
RING = FIRST + WHOLE + HALVES + (("xm", 1, "p", "x2"), ("xp", 2, "m", "x2"))
BOTH = FIRST + WHOLE + HALVES + (("2", 1, "x", "x2"), ("xp", 2, "m", "x2"))


class Gather:
    def __init__(self, plan, buffers, parts, blocks, neighbours, send_sems, recv_sems):
        self.plan = plan
        self.buffers = buffers
        self.parts = parts
        self.blocks = blocks
        self.neighbours = neighbours
        self.send_sems = send_sems
        self.recv_sems = recv_sems
        self.left = set()

    def copies(self, step, arriving):
        name, part, to, there = self.plan[step]
        name = there if arriving else name
        device = self.neighbours[to]
        for b, (buffer, parts) in enumerate(zip(self.buffers, self.parts)):
            view = parts[part](buffer(self.blocks[name]))
            yield pltpu.make_async_remote_copy(
                src_ref=view,
                dst_ref=view,
                send_sem=self.send_sems.at[b, step],
                recv_sem=self.recv_sems.at[b, step],
                device_id=device,
                device_id_type=MESH,
            )

    def send(self, *steps):
        for step in steps:
            for copy in self.copies(step, False):
                copy.start()

    def arrive(self, *steps):
        for step in steps:
            for copy in self.copies(step, True):
                copy.wait_recv()

    def leave(self, *steps):
        for step in steps:
            self.left.add(step)
            for copy in self.copies(step, False):
                copy.wait_send()

    def finish(self):
        self.leave(*(step for step in range(len(self.plan)) if step not in self.left))


def kernel(
    wq_ref, wk_ref, wv_ref, wo_ref, qa_ref, ka_ref, hid_ref, pos_ref, ck_ref, cv_ref, len_ref,
    out_ref,
    qf, qf2, kvf, wq, wq2, kvw, wo_stage, wo, hid, stage, ck, cv, outgoing, outgoing2, incoming, incoming2, att,
    acc, cosine, sine, pick, pick2, unpick, fresh_kv, scores, probs, mixed, main_out, tail_out,
    stage_sems, cache_sems, a_send, a_recv, w_send, w_recv, qkv_send, qkv_recv,
    gq_send, gq_recv, gr_send, gr_recv, go_send, go_recv, ga_send, ga_recv, core_send, core_recv,
):
    r = lax.axis_index("rep")
    t = lax.axis_index("tp")

    x_rep = lax.rem(r + 4, 8)
    base = r // 4 * 4
    other = 4 - base
    z = lax.rem(r, 4)
    zp, zm, z2 = lax.rem(z + 1, 4), lax.rem(z + 3, 4), lax.rem(z + 2, 4)
    rep_blocks = {
        "own": r, "x": x_rep, "p": base + zp, "m": base + zm, "2": base + z2,
        "xp": other + zp, "xm": other + zm, "x2": other + z2,
    }
    rep_neighbours = {"x": (x_rep, t), "p": (base + zp, t), "m": (base + zm, t)}
    side = lax.rem(t // 2, 2)

    def across(other_side, rep):
        return jnp.where(other_side != side, lax.rem(rep + 4, 8), rep)

    y = t // 4
    low = lax.rem(t, 4)
    far = lax.rem(low + 2, 4)
    yp, ym, y2 = lax.rem(y + 1, 4) * 4, lax.rem(y + 3, 4) * 4, lax.rem(y + 2, 4) * 4
    tp_blocks = {
        "own": t, "x": y * 4 + far, "p": yp + low, "m": ym + low, "2": y2 + low,
        "xp": yp + far, "xm": ym + far, "x2": y2 + far,
    }
    tp_neighbours = {k: (r, tp_blocks[k]) for k in ("x", "p", "m")}
    core = t + 1 - 2 * lax.rem(t, 2)
    barrier = pltpu.get_barrier_semaphore()

    def greet(device):
        pl.semaphore_signal(barrier, inc=1, device_id=device, device_id_type=MESH)

    for k in range(1, TP):
        greet((r, lax.rem(t + k, TP)))
    for k in range(1, REP):
        greet((lax.rem(r + k, REP), t))
    for k in range(8):
        greet((x_rep, k // 2 * 4 + 2 - side * 2 + k % 2))

    def hidden_copy(i, slot):
        return pltpu.make_async_copy(
            hid_ref.at[:, :, pl.ds(i * 1024, 1024)], stage.at[slot], stage_sems.at[slot]
        )

    hidden_copy(0, 0).start()
    hidden_copy(1, 1).start()

    factors = []
    for g in range(KVH):
        query_peak = jnp.broadcast_to(
            jnp.max(qa_ref[8 * g : 8 * g + 8, :], axis=0, keepdims=True), (8, HD)
        )
        query_peak = jnp.maximum(query_peak, swap_halves(query_peak))
        key_peak = jnp.broadcast_to(ka_ref[g : g + 1, :], (8, HD))
        key_peak = jnp.maximum(key_peak, swap_halves(key_peak))
        factors.append(jnp.sqrt(key_peak / query_peak)[0:1, :])
    for dst in range(TP):
        for n, folded in enumerate((qf, qf2)):
            at = 256 * dst + HD * n
            folded[dst] = (wq_ref[:, at : at + HD].astype(F32) * factors[dst // 4]).astype(BF)
    for g in range(KVH):
        kvf[g] = (wk_ref[:, HD * g : HD * g + HD].astype(F32) / factors[g]).astype(BF)
        kvf[KVH + g] = wv_ref[:, HD * g : HD * g + HD]

    pl.semaphore_wait(barrier, TP - 1 + REP - 1 + 8)

    def wo_columns(i):
        return wo_ref.at[:, pl.ds(pl.multiple_of(i * 512, 512), 512)]

    def wo_scatter(k, carry):
        to = lax.rem(r + k, REP)
        pltpu.make_async_remote_copy(
            src_ref=wo_columns(across(lax.rem(r, 2), to)), dst_ref=wo_stage.at[r],
            send_sem=w_send.at[0], recv_sem=w_recv.at[0],
            device_id=(to, t), device_id_type=MESH,
        ).start()
        return carry


    half = t // 8
    q_rows = pl.ds(pl.multiple_of(t * ROWS, ROWS), ROWS)
    kv_rows = pl.ds(pl.multiple_of(lax.rem(t, 8) * ROWS, ROWS), ROWS)

    def deliver(k, carry):
        dst = lax.rem(t + k, TP)
        rep = across(lax.rem(dst // 2, 2), r)
        pltpu.make_async_remote_copy(
            src_ref=qf.at[dst], dst_ref=wq.at[rep, q_rows],
            send_sem=a_send.at[0], recv_sem=a_recv.at[0],
            device_id=(rep, dst), device_id_type=MESH,
        ).start()

        @pl.when(lax.rem(dst, 2) == half)
        def _():
            pltpu.make_async_remote_copy(
                src_ref=kvf.at[lax.rem(dst, 4) // 2 * 4 + dst // 4], dst_ref=kvw.at[rep, kv_rows],
                send_sem=a_send.at[1], recv_sem=a_recv.at[1],
                device_id=(rep, dst), device_id_type=MESH,
            ).start()

        return carry

    def deliver_second(k, carry):
        dst = lax.rem(t + k, TP)
        rep = across(lax.rem(dst // 2, 2), r)
        pltpu.make_async_remote_copy(
            src_ref=qf2.at[dst], dst_ref=wq2.at[rep, q_rows],
            send_sem=a_send.at[2], recv_sem=a_recv.at[2],
            device_id=(rep, dst), device_id_type=MESH,
        ).start()
        return carry

    lax.fori_loop(1, TP, deliver, 0)
    pltpu.make_async_copy(qf.at[t], wq.at[r, q_rows], a_recv.at[0]).start()
    own_kv = lax.rem(t, 2) == half

    @pl.when(own_kv)
    def _():
        pltpu.make_async_copy(
            kvf.at[lax.rem(t, 4) // 2 * 4 + t // 4], kvw.at[r, kv_rows], a_recv.at[1]
        ).start()

    lax.fori_loop(1, TP, deliver_second, 0)
    pltpu.make_async_copy(qf2.at[t], wq2.at[r, q_rows], a_recv.at[2]).start()
    lax.fori_loop(1, REP, wo_scatter, 0)
    pltpu.make_async_copy(wo_columns(across(lax.rem(r, 2), r)), wo_stage.at[r], w_recv.at[0]).start()

    wo_rows = pl.ds(pl.multiple_of(lax.rem(t, 8) * ROWS, ROWS), ROWS)

    def wo_deliver(i, carry):
        dst = 2 * i + half
        rep = across(lax.rem(i, 2), r)

        @pl.when(dst != t)
        def _():
            pltpu.make_async_remote_copy(
                src_ref=wo_stage.at[i], dst_ref=wo.at[rep, wo_rows],
                send_sem=w_send.at[1], recv_sem=w_recv.at[1],
                device_id=(rep, dst), device_id_type=MESH,
            ).start()

        @pl.when(dst == t)
        def _():
            pltpu.make_async_copy(wo_stage.at[i], wo.at[r, wo_rows], w_recv.at[1]).start()

        return carry

    cache_copies = [
        pltpu.make_async_copy(ck_ref, ck, cache_sems.at[0]),
        pltpu.make_async_copy(cv_ref, cv, cache_sems.at[1]),
    ]

    def relayout(i, carry):
        slot = lax.rem(i, 2)
        hidden_copy(i, slot).wait()
        block = stage[slot].reshape(ALL_ROWS, 1024)
        for n in range(8):
            at = pl.multiple_of(across(n % 2, i) * 1024 + n * 128, 128)
            hid[:, pl.ds(at, 128)] = block[:, n * 128 : n * 128 + 128]

        @pl.when(i < 6)
        def _():
            hidden_copy(i + 2, slot).start()

        return carry

    gather_q = Gather(
        PAIR,
        [lambda block: wq.at[block], lambda block: kvw.at[block]], [BY_ROWS, BY_ROWS], rep_blocks, rep_neighbours,
        gq_send, gq_recv,
    )
    gather_r = Gather(
        BOTH, [lambda block: wq2.at[block]], [BY_ROWS], rep_blocks, rep_neighbours,
        gr_send, gr_recv,
    )
    gather_o = Gather(
        RING,
        [lambda block: wo.at[block]], [BY_ROWS], rep_blocks, rep_neighbours, go_send, go_recv,
    )
    pltpu.make_async_copy(wq.at[r], wq.at[r], a_recv.at[0]).wait()
    pltpu.make_async_copy(kvw.at[r], kvw.at[r], a_recv.at[1]).wait()
    gather_q.send(0, 1, 2)
    pltpu.make_async_copy(wq2.at[r], wq2.at[r], a_recv.at[2]).wait()
    gather_r.send(0, 1, 2)
    pltpu.make_async_copy(wo_stage, wo_stage, w_recv.at[0]).wait()
    lax.fori_loop(0, REP, wo_deliver, 0)
    for copy in cache_copies:
        copy.start()
    lax.fori_loop(0, 8, relayout, 0)

    place = jnp.sum(
        jnp.where(
            iota((ALL_ROWS, 320), 0) // 2 == iota((ALL_ROWS, 320), 1),
            pos_ref[...].reshape(1, TP * SEQS).astype(F32),
            0.0,
        ),
        axis=1,
        keepdims=True,
    ) + lax.rem(iota((ALL_ROWS, 1), 0), 2).astype(F32)
    channel = lax.rem(iota((1, HD), 1), HD // 2).astype(F32)
    angle = place * (ROPE_THETA ** (-2.0 * channel / HD))
    cosine[...] = jnp.cos(angle)
    sine[...] = jnp.sin(angle) * jnp.where(iota((1, HD), 1) < HD // 2, -1.0, 1.0)

    main_out[...] = jnp.zeros_like(main_out)
    tail_out[...] = jnp.zeros_like(tail_out)

    row, col = iota((416, 320), 0), iota((416, 320), 1)
    order, token = row // 8, lax.rem(row - H_ROWS + 256, 128)
    source = lax.rem(row, 8) // 2 * 80 + 2 * order + lax.rem(row, 2)
    fresh_row = jnp.logical_and(lax.rem(col, 80) == TOKENS + token, token < TOKENS)
    is_key, is_value = row < H_ROWS + 128, col >= 160
    hit = jnp.where(
        row < H_ROWS, (col == source).astype(F32),
        jnp.logical_and(fresh_row, is_key != is_value).astype(F32),
    )
    pick[...] = hit.astype(BF)
    row, col = iota((H_ROWS, 192), 0), iota((H_ROWS, 192), 1)
    source = lax.rem(row, 8) // 2 * 48 + row // 8 * 2 + lax.rem(row, 2)
    pick2[...] = (col == source).astype(F32).astype(BF)
    row, col = iota((H_ROWS, 256), 0), iota((H_ROWS, 256), 1)
    head, token = row // TOKENS, lax.rem(row, TOKENS)
    source = token // 2 * 8 + head * 2 + lax.rem(token, 2)
    unpick[...] = (col == source).astype(F32).astype(BF)

    kv_half = lax.rem(t, 2) * 512

    def project(name, first=False):
        block = rep_blocks[name]
        q_at = pl.multiple_of(block * 1024, 1024)
        kv_at = pl.multiple_of(block * 1024 + kv_half, 512)
        for m in range(0, ALL_ROWS, 128):
            q = jnp.dot(hid[m : m + 128, pl.ds(q_at, 1024)], wq[block], preferred_element_type=F32)
            kv = jnp.dot(hid[m : m + 128, pl.ds(kv_at, 512)], kvw[block], preferred_element_type=F32)
            if first:
                acc[m : m + 128, 0:128] = q
                acc[m : m + 128, 256:384] = kv
            else:
                acc[m : m + 128, 0:128] += q
                acc[m : m + 128, 256:384] += kv

    def project_second(name, first=False):
        block = rep_blocks[name]
        q_at = pl.multiple_of(block * 1024, 1024)
        for m in range(0, ALL_ROWS, 128):
            q = jnp.dot(hid[m : m + 128, pl.ds(q_at, 1024)], wq2[block], preferred_element_type=F32)
            if first:
                acc[m : m + 128, 128:256] = q
            else:
                acc[m : m + 128, 128:256] += q

    is_value_device = lax.rem(t // 2, 2) == 1

    def rotate(x, rows):
        return x * cosine[rows, :] + swap_halves(x) * sine[rows, :]

    def to_owner(buffer, landing, i, k):
        dst = lax.rem(t + k, TP)

        @pl.when(k < TP)
        def _():
            pltpu.make_async_remote_copy(
                src_ref=buffer.at[dst], dst_ref=landing.at[t],
                send_sem=qkv_send.at[i], recv_sem=qkv_recv.at[i],
                device_id=(r, dst), device_id_type=MESH,
            ).start()

        @pl.when(k == TP)
        def _():
            pltpu.make_async_copy(buffer.at[dst], landing.at[t], qkv_recv.at[i]).start()

    def spread(k, carry):
        dst = lax.rem(t + k, TP)
        rows = pl.ds(pl.multiple_of(dst * TOKENS, 8), TOKENS)
        kv = acc[rows, 256:384]
        kv = jnp.where(is_value_device, kv, rotate(kv, rows))
        outgoing[dst] = jnp.concatenate([rotate(acc[rows, 0:128], rows), kv], axis=0).astype(BF)
        to_owner(outgoing, incoming, 0, k)
        return carry

    def spread_second(k, carry):
        dst = lax.rem(t + k, TP)
        rows = pl.ds(pl.multiple_of(dst * TOKENS, 8), TOKENS)
        q = rotate(acc[rows, 128:256], rows)
        outgoing2[dst] = jnp.concatenate([q, jnp.zeros((8, HD), F32)], axis=0).astype(BF)
        to_owner(outgoing2, incoming2, 1, k)
        return carry

    gather_q.arrive(1)
    gather_q.send(5)
    gather_q.arrive(2)
    gather_q.send(6)
    project("own", True)
    project_second("own", True)
    gather_q.leave(5, 6)
    gather_q.arrive(0)
    gather_q.send(3, 4)
    gather_r.arrive(1)
    gather_r.send(5)
    gather_r.arrive(2)
    gather_r.send(6)
    gather_r.arrive(0)
    gather_r.send(3, 4)
    project("m")
    project("p")
    project("x")
    gather_q.arrive(5)
    gather_q.send(7)
    gather_q.arrive(6)
    gather_q.send(8)
    project("2")
    pltpu.make_async_copy(wo.at[r], wo.at[r], w_recv.at[1]).wait()
    gather_o.send(0)
    project_second("m")
    project_second("p")
    project_second("x")
    gather_r.arrive(5)
    gather_r.send(7)
    gather_r.arrive(6)
    gather_q.arrive(3)
    project("xm")
    gather_q.arrive(4)
    project("xp")
    gather_q.arrive(7, 8)
    project("x2")
    lax.fori_loop(1, TP + 1, spread, 0)
    project_second("2")
    gather_r.arrive(3)
    gather_r.arrive(4)
    gather_r.send(8)
    gather_o.send(1, 2)
    project_second("xm")
    project_second("xp")
    gather_r.arrive(7, 8)
    project_second("x2")
    lax.fori_loop(1, TP + 1, spread_second, 0)
    gather_o.arrive(0)
    gather_o.send(3, 4)

    for copy in cache_copies:
        copy.wait()
    lengths = jnp.sum(
        jnp.where(
            iota((H_ROWS, SEQS), 0) // 8 == iota((H_ROWS, SEQS), 1), len_ref[...].astype(F32), 0.0
        ),
        axis=1,
        keepdims=True,
    )
    live = iota((H_ROWS, LMAX), 1).astype(F32) < lengths
    row, col = iota((H_ROWS, 128), 0), iota((H_ROWS, 128), 1)
    fresh_live = jnp.logical_and(row // 8 == col // 2, lax.rem(col, 2) <= lax.rem(row, 2))
    mixed[H_ROWS:256, :] = jnp.zeros((256 - H_ROWS, HD), BF)

    def attend(part, g):
        if part == 0:
            gathered = incoming[pl.ds(g * 4, 4)].reshape(320, HD)
            ordered = jnp.dot(pick[...], gathered, preferred_element_type=F32)
            fresh_kv[g] = ordered[H_ROWS:].astype(BF)
            ordered = ordered[:H_ROWS]
        else:
            gathered = incoming2[pl.ds(g * 4, 4)].reshape(192, HD)
            ordered = jnp.dot(pick2[...], gathered, preferred_element_type=F32)
        key_new, value_new = fresh_kv[g, 0:128], fresh_kv[g, 128:256]
        for b in range(SEQS):
            scores[8 * b : 8 * b + 8, :] = lax.dot_general(
                ordered[8 * b : 8 * b + 8].astype(BF), ck[b, g], (((1,), (1,)), ((), ())),
                preferred_element_type=F32,
            )
        scale = HD ** (-0.5)
        cached = jnp.where(live, scores[...] * scale, -jnp.inf)
        fresh = lax.dot_general(
            ordered.astype(BF), key_new, (((1,), (1,)), ((), ())), preferred_element_type=F32
        )
        fresh = jnp.where(fresh_live, fresh * scale, -jnp.inf)
        top = jnp.maximum(
            jnp.max(cached, axis=1, keepdims=True), jnp.max(fresh, axis=1, keepdims=True)
        )
        cached = jnp.exp(cached - top)
        fresh = jnp.exp(fresh - top)
        total = jnp.sum(cached, axis=1, keepdims=True) + jnp.sum(fresh, axis=1, keepdims=True)
        probs[...] = cached
        fresh_part = jnp.dot(fresh.astype(BF), value_new, preferred_element_type=F32)
        parts = [
            jnp.dot(probs[8 * b : 8 * b + 8, :].astype(BF), cv[b, g], preferred_element_type=F32)
            for b in range(SEQS)
        ]
        mixed[0:H_ROWS, :] = ((jnp.concatenate(parts, axis=0) + fresh_part) / total).astype(BF)
        by_head = jnp.dot(unpick[...], mixed[...], preferred_element_type=F32)
        heads = [by_head[TOKENS * h : TOKENS * h + TOKENS] for h in range(4)]
        last = [x[MAIN:] for x in heads]
        tail = [jnp.concatenate(pair, axis=0) for pair in zip(last[:2], last[2:])]
        at = g % 2 * 1280
        att[t, part * 2 + g // 2, :, at : at + 1280] = jnp.concatenate(
            [x[:16] for x in heads] + [x[16:MAIN] for x in heads] + tail, axis=1
        ).astype(BF)

    names = ("own", "m", "p", "x", "2", "xm", "xp", "x2")
    gathers = [
        Gather(
            PAIR,
            [lambda block, g=g: att.at[block, g]], [BY_LANES], tp_blocks, tp_neighbours,
            ga_send.at[pl.ds(g, 1)], ga_recv.at[pl.ds(g, 1)],
        )
        for g in range(KVH)
    ]

    def to_core(g, name, block):
        i = names.index(name)
        return pltpu.make_async_remote_copy(
            src_ref=att.at[block, g], dst_ref=att.at[block, g],
            send_sem=core_send.at[g, i], recv_sem=core_recv.at[g, i],
            device_id=(r, core), device_id_type=MESH,
        )

    def share(g, *group):
        for name in group:
            to_core(g, name, tp_blocks[name]).start()

    def first_hop(g):
        gather = gathers[g]
        gather.arrive(1)
        gather.send(5)
        gather.arrive(2)
        gather.send(6)
        gather.arrive(0)
        gather.send(3, 4)
        share(g, "m", "p", "x")

    def second_hop(g):
        gather = gathers[g]
        gather.arrive(5)
        gather.send(7)
        gather.arrive(6)
        gather.send(8)
        share(g, "2")

    def third_hop(g):
        gathers[g].arrive(3)
        share(g, "xm")
        gathers[g].arrive(4)
        share(g, "xp")

    pltpu.make_async_copy(incoming, incoming, qkv_recv.at[0]).wait()

    def attend_pair(piece):
        part, first = piece // 2, piece % 2 * 2
        attend(part, first)
        attend(part, first + 1)
        gathers[piece].send(0, 1, 2)
        share(piece, "own")

    attend_pair(0)
    gather_o.arrive(1)
    gather_o.send(5)
    gather_o.arrive(2)
    gather_o.send(6)
    attend_pair(1)
    first_hop(0)
    pltpu.make_async_copy(incoming2, incoming2, qkv_recv.at[1]).wait()
    attend_pair(2)
    first_hop(1)
    second_hop(0)
    attend_pair(3)
    first_hop(2)
    second_hop(1)
    gather_o.arrive(3)
    gather_o.send(7)
    gather_o.arrive(4)
    gather_o.send(8)
    first_hop(3)
    second_hop(2)
    second_hop(3)

    chips = {name: tp_blocks[name] // 2 * 2 for name in names}
    flip = 1 - 2 * lax.rem(t, 2)

    def from_core(*group):
        for name in group:
            for g in range(KVH):
                to_core(g, name, tp_blocks[name] + flip).wait_recv()

    def output(i, group, chunks):
        for chunk in chunks:
            block = rep_blocks[chunk]
            g, side = block // 2, lax.rem(block, 2)
            base = lax.rem(g, 2) * 1280
            rows = [
                jnp.concatenate(
                    [
                        att[
                            pl.ds(chips[name], 2), part * 2 + g // 2, :,
                            pl.ds(pl.multiple_of(base + at + n * 128, 128), 128),
                        ].reshape(32, 128)
                        for n in range(2)
                        for part in range(2)
                    ],
                    axis=1,
                )
                for at in (side * 256, side * 256 + 512, 1024)
                for name in group
            ]
            product = lax.dot_general(
                jnp.concatenate(rows, axis=0), wo[block], (((1,), (1,)), ((), ())),
                preferred_element_type=F32,
            )
            count = 32 * len(group)
            main_out[i, : 2 * count] += product[: 2 * count]
            tail_out[i, side, :count] += product[2 * count :]

    def store(i, group):
        for n, name in enumerate(group):
            rows = []
            for s in (32 * n, 32 * n + 16):
                rows.append(main_out[i, s : s + 16, :])
                rows.append(main_out[i, 32 * len(group) + s : 32 * len(group) + s + 16, :])
                rows.append(tail_out[i, 0, s : s + 8, :] + tail_out[i, 1, s + 8 : s + 16, :])
            at = pl.ds(chips[name] * SEQS, 2 * SEQS)
            out_ref[at] = jnp.concatenate(rows, axis=0).astype(BF).reshape(2 * SEQS, 2, 512)

    near, distant, last = ("own", "m", "p", "x"), ("2", "xm", "xp"), ("x2",)
    chunks = near + distant + last
    from_core(*near)
    output(0, near, ("own", "m", "p", "x", "xm", "xp"))
    for g in range(KVH):
        third_hop(g)
    gather_o.arrive(5, 6)
    output(0, near, ("2",))
    from_core(*distant)
    output(1, distant, chunks[:-1])
    for g in range(KVH):
        gathers[g].arrive(7, 8)
        share(g, "x2")
    from_core(*last)
    output(2, last, chunks[:-1])
    gather_o.arrive(7, 8)
    for i, group in enumerate((near, distant, last)):
        output(i, group, last)
        store(i, group)

    def sent_q(k, carry):
        dst = lax.rem(t + k, TP)
        pltpu.make_async_copy(qf.at[dst], qf.at[dst], a_send.at[0]).wait()
        pltpu.make_async_copy(qf2.at[dst], qf2.at[dst], a_send.at[2]).wait()
        pltpu.make_async_copy(outgoing.at[dst], outgoing.at[dst], qkv_send.at[0]).wait()
        pltpu.make_async_copy(outgoing2.at[dst], outgoing2.at[dst], qkv_send.at[1]).wait()

        @pl.when(lax.rem(dst, 2) == half)
        def _():
            pltpu.make_async_copy(kvf.at[0], kvf.at[0], a_send.at[1]).wait()

        return carry

    lax.fori_loop(1, TP, sent_q, 0)

    def sent_o(i, carry):
        pltpu.make_async_copy(wo_stage.at[i], wo_stage.at[i], w_send.at[0]).wait()
        return carry

    lax.fori_loop(1, REP, sent_o, 0)

    def delivered_o(i, carry):
        @pl.when(2 * i + half != t)
        def _():
            pltpu.make_async_copy(wo_stage.at[i], wo_stage.at[i], w_send.at[1]).wait()

        return carry

    lax.fori_loop(0, REP, delivered_o, 0)
    gather_q.finish()
    gather_r.finish()
    gather_o.finish()
    for g in range(KVH):
        gathers[g].finish()
        for name in names:
            to_core(g, name, tp_blocks[name]).wait_send()


def body(
    query_weight, key_weight, value_weight, output_weight, query_amax, key_amax,
    hidden, positions, cache_keys, cache_values, lengths,
):
    vmem = pl.BlockSpec(memory_space=pltpu.VMEM)
    hbm = pl.BlockSpec(memory_space=pl.ANY)
    dma = pltpu.SemaphoreType.DMA
    result = pl.pallas_call(
        kernel,
        out_shape=jax.ShapeDtypeStruct((TP * SEQS, 2, 512), BF),
        in_specs=[vmem, vmem, vmem, hbm, vmem, vmem, hbm, vmem, hbm, hbm, vmem],
        out_specs=vmem,
        scratch_shapes=[
            pltpu.VMEM((TP, ROWS, HD), BF),
            pltpu.VMEM((TP, ROWS, HD), BF),
            pltpu.VMEM((2 * KVH, ROWS, HD), BF),
            pltpu.VMEM((REP, TP * ROWS, HD), BF),
            pltpu.VMEM((REP, TP * ROWS, HD), BF),
            pltpu.VMEM((REP, 8 * ROWS, HD), BF),
            pltpu.VMEM((REP, ROWS, 512), BF),
            pltpu.VMEM((REP, 512, 512), BF),
            pltpu.VMEM((ALL_ROWS, D), BF),
            pltpu.VMEM((2, 320, 2, 1024), BF),
            pltpu.VMEM((SEQS, KVH, LMAX, HD), BF),
            pltpu.VMEM((SEQS, KVH, LMAX, HD), BF),
            pltpu.VMEM((TP, 80, HD), BF),
            pltpu.VMEM((TP, 48, HD), BF),
            pltpu.VMEM((TP, 80, HD), BF),
            pltpu.VMEM((TP, 48, HD), BF),
            pltpu.VMEM((TP, KVH, 16, 2560), BF),
            pltpu.VMEM((ALL_ROWS, 384), F32),
            pltpu.VMEM((ALL_ROWS, HD), F32),
            pltpu.VMEM((ALL_ROWS, HD), F32),
            pltpu.VMEM((416, 320), BF),
            pltpu.VMEM((H_ROWS, 192), BF),
            pltpu.VMEM((H_ROWS, 256), BF),
            pltpu.VMEM((KVH, 256, HD), BF),
            pltpu.VMEM((H_ROWS, LMAX), F32),
            pltpu.VMEM((H_ROWS, LMAX), F32),
            pltpu.VMEM((256, HD), BF),
            pltpu.VMEM((3, 256, 512), F32),
            pltpu.VMEM((3, 2, 128, 512), F32),
            dma((2,)), dma((2,)), dma((3,)), dma((3,)), dma((2,)), dma((2,)), dma((2,)), dma((2,)),
            dma((2, 9)), dma((2, 9)), dma((1, 9)), dma((1, 9)), dma((1, 9)), dma((1, 9)), dma((KVH, 9)), dma((KVH, 9)),
            dma((KVH, 8)), dma((KVH, 8)),
        ],
        compiler_params=pltpu.CompilerParams(
            collective_id=0, has_side_effects=True, vmem_limit_bytes=62 * 2**20
        ),
    )(
        query_weight, key_weight, value_weight, output_weight,
        query_amax.reshape(HQ, HD), key_amax.reshape(KVH, HD),
        hidden, positions, cache_keys, cache_values, lengths.reshape(1, -1),
    )
    return result


def solution(mesh):
    in_specs = (
        P(("rep", "tp"), None),
        P(("rep", "tp"), None),
        P(("rep", "tp"), None),
        P(("rep", "tp"), None),
        P(),
        P(),
        P("rep", None, None),
        P("rep"),
        P(("rep", "tp"), None, None, None),
        P(("rep", "tp"), None, None, None),
        P(("rep", "tp")),
    )
    out_specs = P("rep", None, "tp")

    def run(*args):
        with jax.sharding.use_abstract_mesh(mesh.abstract_mesh):
            return jax.shard_map(
                body, mesh=mesh, in_specs=in_specs, out_specs=out_specs, check_vma=False
            )(*args)

    return run
```
